128 devices in a mesh: gx: 16 (over z, y), gy: 8 (over x, core).
Axes of the slice: x: 4, y: 4, z: 4, core: 2. Of those that a mesh axis runs over, the one named last changes fastest.
Arguments:
- atm_flux: bfloat16 [128, 128, 1, 16, 256], P(('gx', 'gy')), may hold values from -6 to 6
- owner_map: int32 [128, 128], P(None, ('gx', 'gy')), may hold values from 0 to 127, as said below
- wet_mask: int32 [512, 16], P('gy', 'gx'), may hold values from 0 to 1, as said below
- stem_weight: bfloat16 [200, 16, 2, 2], replicated, may hold values from -0.75 to 0.75
- depth_weight: float32 [2, 200, 7, 7], replicated, may hold values from -0.875 to 0.875
- depth_bias: float32 [2, 200], replicated, may hold values from -3 to 3
- norm_gain: float32 [2, 200], replicated, may hold values from 0.1 to 1.9
- expand_weight: bfloat16 [2, 200, 800], replicated, may hold values from -0.4375 to 0.4375
- expand_bias: float32 [2, 800], replicated, may hold values from -3 to 3
- reduce_weight: bfloat16 [2, 800, 200], replicated, may hold values from -0.21875 to 0.21875
Outputs:
- ocean_state: bfloat16 [200, 512, 2048], P(None, 'gy', 'gx')
The draws below stay inside these ranges and needn't reach their ends.
Inputs may be any that keep to these rules, and one draw needn't show every extreme that they name: For every ocean tile k, the column owner_map[:, k] is a permutation of 0 to 127. Every ocean tile (the 64 rows of wet_mask that one index pair of gx and gy holds) has at most 48 rows equal to 1, and some tile has exactly 48.
All inputs are finite; a program needn't handle non-finite values.
Results may differ from the reference program's by a relative error of at most 0.0062.
Values may be sent and summed in bfloat16 or wider, within the bound.
No kernel may reach another device: no remote copies, remote signals or barrier semaphores. Data moves between devices by JAX's collectives and lax.ppermute only.
A program may use at most 128 MiB of HBM per device.

```python
import jax
import jax.numpy as jnp
from jax import lax

RH = 64
RW = 128
FLUX = 16
WIDTH = 200
HIDDEN_SIZE = 800
BLOCKS = 2
TILES = 128
FRP = 1
LAT = 512
LON = 2048
WET_MOST = 48
N_GX = 16
N_GY = 8


def permute_tiles(subkey):
    return jax.random.permutation(subkey, TILES)


def permute_latitudes(subkey):
    return jax.random.permutation(subkey, RH)


def draw_owner_map(key, part):
    subkeys = jax.random.split(jax.random.fold_in(key, 5), TILES)
    placement = jax.vmap(permute_tiles)(subkeys)
    return jnp.transpose(placement).astype(jnp.int32)


def draw_wet_mask(key, part):
    count_key = jax.random.fold_in(key, 11)
    pick_key = jax.random.fold_in(key, 12)
    order_key = jax.random.fold_in(key, 13)
    counts = jax.random.randint(count_key, (TILES,), 1, WET_MOST + 1)
    forced = jax.random.randint(pick_key, (), 0, TILES)
    counts = jnp.where(jnp.arange(TILES) == forced, WET_MOST, counts)
    ranks = jax.vmap(permute_latitudes)(jax.random.split(order_key, TILES))
    wet = (ranks < counts[:, None]).astype(jnp.int32)
    wet = wet.reshape(N_GX, N_GY, RH)
    return jnp.transpose(wet, (1, 2, 0)).reshape(N_GY * RH, N_GX).astype(jnp.int32)


def level_of(key, dims, cuts, least, high):
    level = 1.0
    for axis_at, shards_of in cuts:
        heights = jax.random.uniform(jax.random.fold_in(jax.random.fold_in(key, 6), axis_at), (shards_of,), jnp.float32, least / len(cuts), high / len(cuts))
        level = level * jnp.repeat(jnp.exp(heights), dims[axis_at] // shards_of).reshape((-1,) + (1,) * (len(dims) - 1 - axis_at))
    return level


def scatter_about(stream_key, extent, scale, limit, cuts=(), held_as=jnp.bfloat16):
    entries = scale * jax.random.normal(stream_key, extent, jnp.float32)
    if cuts:
        entries = entries * level_of(stream_key, extent, cuts, -0.22, 0.18)
    return jnp.clip(entries, -limit, limit).astype(held_as)


def setup_inputs(seed: int = 0) -> dict:
    keys = jax.random.split(jax.random.key(seed), 11)
    atm_flux = scatter_about(keys[0], (TILES, TILES, FRP, FLUX, 2 * RW), 1.0, 6.0, ((0, 128),))
    owner_map = draw_owner_map(jax.random.fold_in(keys[10], 71), 0)
    wet_mask = draw_wet_mask(jax.random.fold_in(keys[10], 71), 0)
    stem_weight = scatter_about(keys[3], (WIDTH, FLUX, 2, 2), (4 * FLUX) ** -0.5, 0.75)
    depth_weight = scatter_about(keys[4], (BLOCKS, WIDTH, 7, 7), 49 ** -0.5, 0.875, (), jnp.float32)
    depth_bias = scatter_about(keys[5], (BLOCKS, WIDTH), 0.5, 3.0, (), jnp.float32)
    norm_gain = jnp.clip(1.0 + 0.18 * jax.random.normal(keys[6], (BLOCKS, WIDTH), jnp.float32), 0.1, 1.9)
    expand_weight = scatter_about(keys[7], (BLOCKS, WIDTH, HIDDEN_SIZE), WIDTH ** -0.5, 0.4375)
    expand_bias = scatter_about(keys[8], (BLOCKS, HIDDEN_SIZE), 0.5, 3.0, (), jnp.float32)
    reduce_weight = scatter_about(keys[9], (BLOCKS, HIDDEN_SIZE, WIDTH), HIDDEN_SIZE ** -0.5, 0.21875)
    return {"atm_flux": atm_flux, "owner_map": owner_map, "wet_mask": wet_mask, "stem_weight": stem_weight, "depth_weight": depth_weight, "depth_bias": depth_bias, "norm_gain": norm_gain, "expand_weight": expand_weight, "expand_bias": expand_bias, "reduce_weight": reduce_weight}


def depth_channel(inputs):
    padded_channel, kernel, offset = inputs
    total = jnp.zeros((LAT, LON), jnp.float32) + offset
    for tap_row in range(7):
        for tap_col in range(7):
            window = padded_channel[tap_row:tap_row + LAT, tap_col:tap_col + LON].astype(jnp.float32)
            total = total + window * kernel[tap_row, tap_col]
    return total

def channel_mix(depth_rows, gain, expand_weight, expand_bias, reduce_weight):
    width = depth_rows.shape[0]
    flat = depth_rows.reshape(width, -1)
    center = lax.optimization_barrier(jnp.mean(flat, axis=0, keepdims=True))
    spread = lax.optimization_barrier(jnp.mean((flat - center) ** 2, axis=0, keepdims=True))
    normed = lax.optimization_barrier(((flat - center) * lax.rsqrt(spread + 1e-06) * gain[:, None]).astype(jnp.bfloat16))
    hidden = jnp.einsum('ch,cn->hn', expand_weight.astype(jnp.float32), normed.astype(jnp.float32)) + expand_bias[:, None]
    hidden = lax.optimization_barrier(jax.nn.gelu(hidden, approximate=True).astype(jnp.bfloat16))
    branch = jnp.einsum('hc,hn->cn', reduce_weight.astype(jnp.float32), hidden.astype(jnp.float32))
    return branch.reshape(depth_rows.shape)

def reference(atm_flux, owner_map, wet_mask, stem_weight, depth_weight, depth_bias, norm_gain, expand_weight, expand_bias, reduce_weight):
    tile_count = N_GX * N_GY
    columns = jnp.arange(tile_count, dtype=jnp.int32)
    sources = jnp.broadcast_to(columns[:, None], (tile_count, tile_count)).astype(jnp.int32)
    inverse = jnp.zeros((tile_count, tile_count), jnp.int32).at[owner_map, columns[None, :]].set(sources)
    placed = atm_flux[inverse, columns[None, :]]
    placed = placed.reshape(tile_count, N_GX, N_GY, FRP, FLUX, 2 * RW)
    fine = jnp.transpose(placed, (2, 0, 3, 4, 1, 5)).reshape(LAT, 2, FLUX, LON, 2)
    stem = jnp.einsum('idkjc,okdc->oij', fine.astype(jnp.float32), stem_weight.astype(jnp.float32))
    cell_mask = jnp.repeat(wet_mask.astype(jnp.float32), RW, axis=1)
    state = lax.optimization_barrier((stem * cell_mask[None]).astype(jnp.bfloat16))
    band = 8
    band_count = LAT // band
    mask_bands = cell_mask.reshape(band_count, band, LON)
    for block_index in range(BLOCKS):
        lon_pad = jnp.concatenate([state[:, :, -3:], state, state[:, :, :3]], axis=2)
        folded = lon_pad[:, LAT - 3:, :][:, ::-1, ::-1]
        bottom = jnp.zeros((WIDTH, 3, LON + 6), jnp.bfloat16)
        padded = jnp.concatenate([bottom, lon_pad, folded], axis=1)
        depth_out = lax.map(depth_channel, (padded, depth_weight[block_index], depth_bias[block_index]))
        depth_bands = jnp.transpose(depth_out.reshape(WIDTH, band_count, band, LON), (1, 0, 2, 3))
        state_bands = jnp.transpose(state.reshape(WIDTH, band_count, band, LON), (1, 0, 2, 3))

        def one_band(inputs):
            depth_rows, state_rows, mask_rows = inputs
            branch = channel_mix(depth_rows, norm_gain[block_index], expand_weight[block_index], expand_bias[block_index], reduce_weight[block_index])
            return ((state_rows.astype(jnp.float32) + branch) * mask_rows[None]).astype(jnp.bfloat16)
        updated = lax.map(one_band, (depth_bands, state_bands, mask_bands))
        state = lax.optimization_barrier(jnp.transpose(updated, (1, 0, 2, 3)).reshape(WIDTH, LAT, LON))
    return state
```

```python
import functools

import jax
import jax.numpy as jnp
import numpy as np
from jax import lax
from jax.experimental import pallas as pl
from jax.experimental.pallas import tpu as pltpu
from jax.sharding import PartitionSpec as P

LANES = 128
GROUP = 8
HALF = LANES // 2
ROOT = float(np.sqrt(2.0 / np.pi))
VMEM_BYTES = 56 * 1024 * 1024
BF16 = jnp.bfloat16
F32 = jnp.float32


def fourier_tables():
    spot = np.arange(LANES)[:, None]
    wave = np.arange(HALF)[None, :]
    angle = 2.0 * np.pi * (spot * wave % LANES) / LANES
    cos, sin = np.cos(angle), np.sin(angle)
    plain = np.concatenate([cos, -sin], axis=1)
    plain[:, HALF] = np.where(np.arange(LANES) % 2 == 0, 1.0, -1.0)
    swapped = np.concatenate([-sin, cos], axis=1)
    swapped[:, 0] = 0.0
    swapped[:, HALF] = 0.0
    forward = np.concatenate([plain, swapped], axis=1)
    inverse = plain.T * (2.0 / LANES)
    inverse[0] /= 2.0
    inverse[HALF] /= 2.0
    edges = np.zeros((LANES, LANES))
    for j in range(3):
        edges[j, j] = 1.0
        edges[4 + j, LANES - 3 + j] = 1.0
    edges[3, :] = 1.0
    edges[7, :] = 1.0
    inverse = np.concatenate([inverse, edges], axis=0)
    return forward, inverse


def deinterleave_table():
    table = np.zeros((2 * LANES, 2 * LANES))
    spot = np.arange(LANES)
    table[2 * spot, spot] = 1.0
    table[2 * spot + 1, LANES + spot] = 1.0
    return table


def fold_table():
    table = np.zeros((LANES, LANES))
    spot = np.arange(LANES - 1)
    table[LANES - 2 - spot, spot] = 1.0
    return table


def dot(left, right):
    return jnp.dot(left, right, preferred_element_type=F32)


def lane_ids(shape):
    return lax.broadcasted_iota(jnp.int32, shape, len(shape) - 1)


def pack_edges(value, row, low_ref, high_ref):
    group = row // 32
    start = 4 * (row % 32)
    lane = lane_ids(value.shape)
    hit = (lane >= start) & (lane < start + 3)
    low = pltpu.roll(value, start, 1)
    high = pltpu.roll(value, lax.rem(start + 3, LANES), 1)
    low_ref[group] = jnp.where(hit, low, low_ref[group])
    high_ref[group] = jnp.where(hit, high, high_ref[group])


def stem_kernel(rows_ref, inverse_ref, arrived_ref, table_ref, weight_ref, state_ref, low_ref, high_ref,
                split_ref):
    pieces = arrived_ref.shape[0]
    flux = arrived_ref.shape[1]
    height = state_ref.shape[0]
    step = 16

    def split(index, _):
        part = arrived_ref[pl.ds(index * step, step)].reshape(step * flux, 2 * LANES)
        split_ref[pl.ds(index * step, step)] = dot(part, table_ref[...]).astype(BF16).reshape(step, flux, 2 * LANES)
        return 0

    lax.fori_loop(0, pieces // step, split, 0)
    state_ref[...] = jnp.zeros_like(state_ref)
    low_ref[...] = jnp.zeros_like(low_ref)
    high_ref[...] = jnp.zeros_like(high_ref)

    def pair(index, _):
        rows = [rows_ref[1 + GROUP * index + at] for at in range(GROUP)]
        columns = []
        for row in rows:
            one = split_ref[inverse_ref[2 * row]]
            two = split_ref[inverse_ref[2 * row + 1]]
            columns.append(jnp.concatenate([one[:, :LANES], one[:, LANES:], two[:, :LANES], two[:, LANES:]], axis=0))
        out = dot(weight_ref[...], jnp.concatenate(columns, axis=1))
        for at, row in enumerate(rows):
            value = out[:, at * LANES:(at + 1) * LANES].astype(BF16)
            state_ref[row] = value
            pack_edges(value, row, low_ref, high_ref)
        return 0

    @pl.when(rows_ref[0] > 0)
    def _():
        lax.fori_loop(0, (rows_ref.shape[0] - 1) // GROUP, pair, 0)


def block_kernel(last, rows_ref, flags_ref, state_ref, south_ref, north_ref, fold_ref, left_ref, right_ref,
                 mix_ref, forward_ref, flipped_ref, inverse_ref, turn_ref, left_weight_ref, right_weight_ref,
                 bias_ref, gain_ref, expand_ref, reduce_ref, *rest):
    if last:
        out_ref, wave_ref, prod_ref, edge_ref, grid_ref, normed_ref, held_ref = rest
    else:
        out_ref, low_ref, high_ref, wave_ref, prod_ref, edge_ref, grid_ref, normed_ref = rest
    height, width, _ = state_ref.shape
    channels = 200
    groups = (rows_ref.shape[0] - 1) // GROUP
    count = rows_ref[0]
    fold = flags_ref[0]

    def transform(index, _):
        part = state_ref[pl.ds(index * 16, 16)].reshape(16 * width, LANES)
        wave_ref[pl.ds(3 + index * 16, 16)] = dot(part, forward_ref[...]).astype(BF16).reshape(16, width, 2 * LANES)
        return 0

    lax.fori_loop(0, height // 16, transform, 0)
    wave_ref[0:3] = dot(south_ref[0:3].reshape(3 * width, LANES), forward_ref[...]).astype(BF16).reshape(3, width, 2 * LANES)

    for side, ref in enumerate((left_ref, right_ref)):
        grid_ref[side, 0] = south_ref[3 + side]
        grid_ref[side, 1] = ref[0]
        grid_ref[side, 2] = ref[1]

    @pl.when(fold == 0)
    def _():
        wave_ref[height + 3:height + 6] = dot(north_ref[0:3].reshape(3 * width, LANES), forward_ref[...]).astype(BF16).reshape(3, width, 2 * LANES)
        grid_ref[0, 3] = north_ref[3]
        grid_ref[1, 3] = north_ref[4]

    @pl.when(fold != 0)
    def _():
        for m in range(3):
            wave_ref[height + 3 + m] = dot(fold_ref[2 - m], flipped_ref[...]).astype(BF16)
        grid_ref[0, 3] = dot(fold_ref[4], turn_ref[...]).astype(BF16)
        grid_ref[1, 3] = dot(fold_ref[3], turn_ref[...]).astype(BF16)

    def corrections(index, _):
        span = pl.ds(pl.multiple_of(index * 16, 16), 16)
        lane = lane_ids((16, LANES))
        for side in range(2):
            weight_ref = (left_weight_ref, right_weight_ref)[side]
            totals = [jnp.where(lane % 4 == 3, bias_ref[side, span], 0.0)] * 2
            slabs = [grid_ref[side, k, span] for k in range(4)]
            for tap_row in range(7):
                terms = [None, None]
                for tap in range(3):
                    shift = 4 * (tap_row - 3) + (tap if side == 0 else -tap)
                    weight = weight_ref[tap_row * 3 + tap, span]
                    moved = [pltpu.roll(slab, -shift % LANES, 1) if shift else slab for slab in slabs]
                    for group in range(2):
                        value = moved[group + 1]
                        if shift > 0:
                            value = jnp.where(lane < LANES - shift, value, moved[group + 2])
                        if shift < 0:
                            value = jnp.where(lane >= -shift, value, moved[group])
                        value = weight * value
                        terms[group] = value if terms[group] is None else terms[group] + value
                totals = [total + term.astype(F32) for total, term in zip(totals, terms)]
            for group in range(2):
                edge_ref[side, group, span] = totals[group].astype(BF16)
        return 0

    lax.fori_loop(0, width // 16, corrections, 0)

    def channel_band(band, _):
        span = pl.ds(pl.multiple_of(band * 16, 16), 16)
        weights = [mix_ref[tap, span] for tap in range(7)]

        def some_rows(index, _):
            for at in range(GROUP):
                spot = index * GROUP + at
                row = rows_ref[1 + spot]
                terms = []
                for tap in range(7):
                    wave = wave_ref[row + tap, span]
                    terms.append(wave[:, :LANES] * weights[tap][:, :LANES])
                    terms.append(wave[:, LANES:] * weights[tap][:, LANES:])
                while len(terms) > 1:
                    terms = [a + b for a, b in zip(terms[::2], terms[1::2])] + terms[len(terms) - len(terms) % 2:]
                prod_ref[spot, span] = terms[0]
            return 0

        lax.fori_loop(0, groups, some_rows, 0)
        return 0

    lax.fori_loop(0, width // 16, channel_band, 0)

    if last:
        held_ref[...] = jnp.zeros_like(held_ref)
    else:
        out_ref[...] = jnp.zeros_like(out_ref)
        low_ref[...] = jnp.zeros_like(low_ref)
        high_ref[...] = jnp.zeros_like(high_ref)

    def normalise(index, slot):
        rows = [rows_ref[1 + GROUP * index + at] for at in range(GROUP)]
        lane = lane_ids((width, LANES))
        joined = []
        for at, row in enumerate(rows):
            group = row // 32
            turn = lax.rem(LANES - 4 * (row % 32), LANES)
            left = pltpu.roll(edge_ref[0, group], turn, 1)
            right = pltpu.roll(edge_ref[1, group], lax.rem(turn + 4, LANES), 1)
            joined.append(jnp.concatenate([prod_ref[GROUP * index + at], jnp.where(lane < 4, left, right)], axis=1))
        depth = dot(jnp.concatenate(joined, axis=0), inverse_ref[...])
        for at in range(GROUP):
            real = depth[at * width:at * width + channels]
            center = jnp.mean(real, axis=0, keepdims=True)
            real = real - center
            spread = jnp.mean(real * real, axis=0, keepdims=True)
            normed = real * lax.rsqrt(spread + 1e-06) * gain_ref[...]
            normed = jnp.concatenate([normed, jnp.ones((width - channels, LANES), F32)], axis=0).astype(BF16)
            normed_ref[slot, :, at * LANES:(at + 1) * LANES] = normed

    def pointwise(index, slot):
        half = dot(expand_ref[...], normed_ref[slot])
        half = half.astype(GELU)
        bend = jnp.tanh(half * (half * half * GELU(8.0 * 0.044715 * ROOT) + GELU(2.0 * ROOT)))
        hidden = (half + half * bend).astype(BF16)
        branch = dot(reduce_ref[...], hidden)
        for at in range(GROUP):
            row = rows_ref[1 + GROUP * index + at]
            value = branch[:, at * LANES:(at + 1) * LANES] + state_ref[row].astype(F32)
            if last:
                held_ref[pl.ds(row, channels, stride=height), :] = value[:channels]
            else:
                value = value.astype(BF16)
                out_ref[row] = value
                pack_edges(value, row, low_ref, high_ref)

    def mix(index, _):
        normalise(2 * index, 0)
        pointwise(2 * index, 0)
        normalise(2 * index + 1, 1)
        pointwise(2 * index + 1, 1)
        return 0

    @pl.when(count > 0)
    def _():
        lax.fori_loop(0, groups // 2, mix, 0)

    if last:
        def finish(index, _):
            out_ref[pl.ds(index * 8, 8)] = held_ref[pl.ds(index * 8 * height, 8 * height), :].astype(BF16).reshape(8, height, LANES)
            return 0

        lax.fori_loop(0, channels // 8, finish, 0)


GELU = jnp.bfloat16


def smem():
    return pl.BlockSpec(memory_space=pltpu.SMEM)


def vmem():
    return pl.BlockSpec(memory_space=pltpu.VMEM)


def run_stem(rows, inverse, arrived, table, weight, height, width):
    return pl.pallas_call(
        stem_kernel,
        out_shape=[
            jax.ShapeDtypeStruct((height, width, LANES), BF16),
            jax.ShapeDtypeStruct((2, width, LANES), BF16),
            jax.ShapeDtypeStruct((2, width, LANES), BF16),
        ],
        in_specs=[smem(), smem(), vmem(), vmem(), vmem()],
        out_specs=[vmem()] * 3,
        scratch_shapes=[
            pltpu.VMEM(arrived.shape, BF16),
        ],
        compiler_params=pltpu.CompilerParams(vmem_limit_bytes=VMEM_BYTES),
        name="stem",
    )(rows, inverse, arrived, table, weight)


def run_block(last, rows, flags, state, *arrays):
    height, width, _ = state.shape
    edge = jax.ShapeDtypeStruct((2, width, LANES), BF16)
    if last:
        out_shape = [jax.ShapeDtypeStruct((200, height, LANES), BF16)]
        extra = [pltpu.VMEM((200 * height, LANES), F32)]
    else:
        out_shape = [jax.ShapeDtypeStruct(state.shape, BF16), edge, edge]
        extra = []
    return pl.pallas_call(
        functools.partial(block_kernel, last),
        out_shape=out_shape,
        in_specs=[smem(), smem()] + [vmem()] * (1 + len(arrays)),
        out_specs=[vmem()] * len(out_shape),
        scratch_shapes=[
            pltpu.VMEM((height + 6, width, 2 * LANES), BF16),
            pltpu.VMEM((rows.shape[0] - 1, width, LANES), BF16),
            pltpu.VMEM((2, 2, width, LANES), BF16),
            pltpu.VMEM((2, 4, width, LANES), BF16),
            pltpu.VMEM((2, width, GROUP * LANES), BF16),
        ] + extra,
        compiler_params=pltpu.CompilerParams(vmem_limit_bytes=VMEM_BYTES),
        name="block",
    )(rows, flags, state, *arrays)


def wet_rows(wet, most):
    height = wet.shape[0]
    count = jnp.sum(wet)
    rank = jnp.cumsum(wet) - 1
    spot = jnp.minimum(jnp.arange(most), count - 1)
    hits = (rank[None, :] == spot[:, None]) & (wet[None, :] > 0)
    rows = jnp.sum(jnp.where(hits, jnp.arange(height)[None, :], 0), axis=1)
    return jnp.concatenate([count[None], rows]).astype(jnp.int32)


def block_weights(depth_weight, depth_bias, norm_gain, expand_weight, expand_bias, reduce_weight, width):
    channels = depth_weight.shape[0]
    spare = width - channels
    taps = jnp.pad(depth_weight, ((0, spare), (0, 0), (0, 0)))
    angle = 2.0 * np.pi * np.arange(HALF + 1)[None, :] * (np.arange(7)[:, None] - 3) / LANES
    cos, sin = np.cos(angle), np.sin(angle)
    real = np.concatenate([cos[:, :HALF], cos[:, HALF:], cos[:, 1:HALF]], axis=1)
    none = np.zeros((7, 1))
    imag = np.concatenate([none, -sin[:, 1:HALF], none, sin[:, 1:HALF]], axis=1)
    table = jnp.asarray(np.concatenate([real, imag], axis=1), F32)
    mix = jnp.einsum("cuv,vk->uck", taps, table, precision=lax.Precision.HIGHEST).astype(BF16)
    phase = np.arange(LANES) % 4
    left = np.stack([(phase + t <= 2) for t in range(3)]).astype(np.float32)
    right = np.stack([(phase >= t) & (phase <= 2) for t in range(3)]).astype(np.float32)
    by_tap = jnp.transpose(taps, (1, 2, 0))
    left_weight = (by_tap[:, :3, :, None] * left[None, :, None, :]).reshape(21, width, LANES).astype(BF16)
    right_weight = (by_tap[:, 6:3:-1, :, None] * right[None, :, None, :]).reshape(21, width, LANES).astype(BF16)
    bias = jnp.pad(depth_bias, (0, spare))
    high = bias.astype(BF16).astype(F32)
    bias = jnp.broadcast_to(jnp.stack([high, bias - high])[:, :, None], (2, width, LANES))
    gain = jnp.broadcast_to(norm_gain[:, None], (channels, LANES))
    half_bias = 0.5 * expand_bias
    high = half_bias.astype(BF16)
    low = (half_bias - high.astype(F32)).astype(BF16)
    expand = jnp.concatenate(
        [(expand_weight.T * BF16(0.5)), high[:, None], low[:, None], jnp.zeros((expand_weight.shape[1], spare - 2), BF16)], axis=1
    )
    reduce = jnp.pad(reduce_weight.T, ((0, spare), (0, 0)))
    return mix, left_weight, right_weight, bias, gain, expand, reduce


def body(
    atm_flux,
    owner_map,
    wet_mask,
    stem_weight,
    depth_weight,
    depth_bias,
    norm_gain,
    expand_weight,
    expand_bias,
    reduce_weight,
):
    lon_count = lax.axis_size("gx")
    lat_count = lax.axis_size("gy")
    lat_index = lax.axis_index("gy")
    channels = depth_weight.shape[1]
    width = (channels + 15) // 16 * 16
    height = wet_mask.shape[0]
    arrived = lax.all_to_all(atm_flux[0], ("gx", "gy"), split_axis=0, concat_axis=0, tiled=True)[:, 0]
    pieces = owner_map.shape[0]
    owner = owner_map[:, 0]
    inverse = jnp.sum(
        jnp.where(owner[None, :] == jnp.arange(pieces)[:, None], jnp.arange(pieces)[None, :], 0), axis=1
    ).astype(jnp.int32)
    rows = wet_rows(wet_mask[:, 0], 48)
    flags = (lat_index == lat_count - 1).astype(jnp.int32)[None]
    stem = jnp.transpose(stem_weight, (0, 2, 3, 1)).reshape(channels, -1)
    stem = jnp.pad(stem, ((0, width - channels), (0, 0)))
    forward, back = fourier_tables()
    flipped = jnp.asarray(forward[::-1], BF16)
    forward = jnp.asarray(forward, BF16)
    back = jnp.asarray(back, BF16)
    turn = jnp.asarray(fold_table(), BF16)
    state, low, high = run_stem(rows, inverse, arrived, jnp.asarray(deinterleave_table(), BF16), stem, height, width)
    east = [(i, (i + 1) % lon_count) for i in range(lon_count)]
    west = [(b, a) for a, b in east]
    up = [(i, i + 1) for i in range(lat_count - 1)]
    down = [(b, a) for a, b in up]
    top = lat_count - 1
    over = [(i * lat_count + top, (lon_count - 1 - i) * lat_count + top) for i in range(lon_count)]
    blocks = depth_weight.shape[0]
    for index in range(blocks):
        last = index == blocks - 1
        mix, left_weight, right_weight, bias, gain, expand, reduce = block_weights(
            depth_weight[index], depth_bias[index], norm_gain[index], expand_weight[index], expand_bias[index],
            reduce_weight[index], width,
        )
        left = lax.ppermute(high, "gx", east) - high
        right = lax.ppermute(low, "gx", west) - low
        upper = jnp.concatenate([state[height - 3:], left[1:], right[1:]])
        lower = jnp.concatenate([state[:3], left[:1], right[:1]])
        south = lax.ppermute(upper, "gy", up)
        north = lax.ppermute(lower, "gy", down)
        mirrored = lax.ppermute(upper, ("gx", "gy"), over)
        out = run_block(
            last, rows, flags, state, south, north, mirrored, left, right, mix, forward, flipped, back, turn,
            left_weight, right_weight, bias, gain, expand, reduce,
        )
        if last:
            return out[0]
        state, low, high = out


def solution(mesh):
    return jax.shard_map(
        body,
        mesh=mesh,
        in_specs=(
            P(("gx", "gy"), None, None, None, None),
            P(None, ("gx", "gy")),
            P("gy", "gx"),
            P(),
            P(),
            P(),
            P(),
            P(),
            P(),
            P(),
        ),
        out_specs=P(None, "gy", "gx"),
        check_vma=False,
    )
```

```python
import functools

import jax
import jax.numpy as jnp
import numpy as np
from jax import lax
from jax.experimental import pallas as pl
from jax.experimental.pallas import tpu as pltpu
from jax.sharding import PartitionSpec as P

LANES = 128
GROUP = 8
HALF = LANES // 2
ROOT = float(np.sqrt(2.0 / np.pi))
BF16 = jnp.bfloat16
F32 = jnp.float32


def fourier_tables():
    spot = np.arange(LANES)[:, None]
    wave = np.arange(HALF)[None, :]
    angle = 2.0 * np.pi * (spot * wave % LANES) / LANES
    cos, sin = np.cos(angle), np.sin(angle)
    plain = np.concatenate([cos, -sin], axis=1)
    plain[:, HALF] = np.where(np.arange(LANES) % 2 == 0, 1.0, -1.0)
    swapped = np.concatenate([-sin, cos], axis=1)
    swapped[:, 0] = 0.0
    swapped[:, HALF] = 0.0
    forward = np.concatenate([plain, swapped], axis=1)
    inverse = plain.T * (2.0 / LANES)
    inverse[0] /= 2.0
    inverse[HALF] /= 2.0
    edges = np.zeros((LANES, LANES))
    for j in range(3):
        edges[j, j] = 1.0
        edges[4 + j, LANES - 3 + j] = 1.0
    edges[3, :] = 1.0
    edges[7, :] = 1.0
    inverse = np.concatenate([inverse, edges], axis=0)
    return forward, inverse


def deinterleave_table():
    table = np.zeros((2 * LANES, 2 * LANES))
    spot = np.arange(LANES)
    table[2 * spot, spot] = 1.0
    table[2 * spot + 1, LANES + spot] = 1.0
    return table


def fold_table():
    table = np.zeros((LANES, LANES))
    spot = np.arange(LANES - 1)
    table[LANES - 2 - spot, spot] = 1.0
    return table


def dot(left, right):
    return jnp.dot(left, right, preferred_element_type=F32)


def lane_ids(shape):
    return lax.broadcasted_iota(jnp.int32, shape, len(shape) - 1)


def pack_edges(value, row, low_ref, high_ref):
    place = (row + 16) % 64
    group = place // 32
    start = 4 * (place % 32)
    lane = lane_ids(value.shape)
    hit = (lane >= start) & (lane < start + 3)
    low = pltpu.roll(value, start, 1)
    high = pltpu.roll(value, lax.rem(start + 3, LANES), 1)
    low_ref[group] = jnp.where(hit, low, low_ref[group])
    high_ref[group] = jnp.where(hit, high, high_ref[group])


def send_edges(flags_ref, state_ref, low_ref, high_ref, row_refs, column_refs):
    height = state_ref.shape[0]
    even_row = flags_ref[0] == 0
    even_column = flags_ref[1] == 0
    row_refs[0][...] = state_ref[pl.ds(jnp.where(even_row, height - 3, 0), 3)]
    row_refs[1][...] = state_ref[pl.ds(jnp.where(even_row, 0, height - 3), 3)]
    column_refs[0][...] = jnp.where(even_column, high_ref[...], low_ref[...])
    column_refs[1][...] = jnp.where(even_column, low_ref[...], high_ref[...])


def prepare_kernel(blocks, coef_ref, table_ref, *outs):
    for block in range(blocks):
        mix_ref, side_ref, gain_ref, bias_ref = outs[4 * block:4 * block + 4]
        coef = coef_ref[block]
        for tap in range(7):
            mix_ref[tap] = dot(coef, table_ref[:, tap * 256:(tap + 1) * 256]).astype(BF16)
        for pair in range(21):
            out = dot(coef, table_ref[:, 1792 + pair * 256:2048 + pair * 256]).astype(BF16)
            side_ref[2 * pair] = out[:, :LANES]
            side_ref[2 * pair + 1] = out[:, LANES:]
        out = dot(coef, table_ref[:, 7168:7552])
        gain_ref[...] = out[:, :LANES]
        bias_ref[0] = out[:, LANES:2 * LANES]
        bias_ref[1] = out[:, 2 * LANES:]


def prepare_table():
    table = np.zeros((160, 7552))
    angle = 2.0 * np.pi * np.arange(HALF + 1)[None, :] * (np.arange(7)[:, None] - 3) / LANES
    cos, sin = np.cos(angle), np.sin(angle)
    none = np.zeros((7, 1))
    real = np.concatenate([cos, cos[:, 1:HALF]], axis=1)
    imag = np.concatenate([none, -sin[:, 1:HALF], none, sin[:, 1:HALF]], axis=1)
    wave = np.concatenate([real, imag], axis=1)
    wave_high = wave.astype(BF16).astype(np.float64)
    phase = np.arange(LANES) % 4
    for row in range(7):
        for tap in range(7):
            spot = row * 7 + tap
            table[spot, row * 256:(row + 1) * 256] = wave_high[tap]
            table[49 + spot, row * 256:(row + 1) * 256] = wave_high[tap]
            table[98 + spot, row * 256:(row + 1) * 256] = wave[tap] - wave_high[tap]
        for tap in range(3):
            at = 1792 + (row * 3 + tap) * LANES
            for copy in (0, 49):
                table[copy + row * 7 + tap, at:at + LANES] = phase + tap <= 2
                table[copy + row * 7 + 6 - tap, at + 2688:at + 2688 + LANES] = (phase >= tap) & (phase <= 2)
    table[147:150, 7168:7296] = 1.0
    table[150, 7296:7424] = 1.0
    table[151, 7424:7552] = 1.0
    return table


def stem_kernel(rows_ref, flags_ref, inverse_ref, arrived_ref, table_ref, weight_ref, state_ref, row_even_ref,
                row_odd_ref, column_even_ref, column_odd_ref, split_ref, low_ref, high_ref):
    pieces = arrived_ref.shape[0]
    flux = arrived_ref.shape[1]
    step = 32

    def split(index, _):
        part = arrived_ref[pl.ds(index * step, step)].reshape(step * flux, 2 * LANES)
        split_ref[pl.ds(index * step, step)] = dot(part, table_ref[...]).astype(BF16).reshape(step, flux, 2 * LANES)
        return 0

    lax.fori_loop(0, pieces // step, split, 0)
    state_ref[...] = jnp.zeros_like(state_ref)
    low_ref[...] = jnp.zeros_like(low_ref)
    high_ref[...] = jnp.zeros_like(high_ref)

    def group(index, _):
        rows = [rows_ref[1 + GROUP * index + at] for at in range(GROUP)]
        columns = []
        for row in rows:
            one = split_ref[inverse_ref[2 * row]]
            two = split_ref[inverse_ref[2 * row + 1]]
            columns.append(jnp.concatenate([one[:, :LANES], one[:, LANES:], two[:, :LANES], two[:, LANES:]], axis=0))
        out = dot(weight_ref[...], jnp.concatenate(columns, axis=1))
        for at, row in enumerate(rows):
            value = out[:, at * LANES:(at + 1) * LANES].astype(BF16)
            state_ref[row] = value
            pack_edges(value, row, low_ref, high_ref)
        return 0

    @pl.when(rows_ref[0] > 0)
    def _():
        lax.fori_loop(0, MOST // GROUP, group, 0)

    send_edges(flags_ref, state_ref, low_ref, high_ref, (row_even_ref, row_odd_ref), (column_even_ref, column_odd_ref))


def transform_kernel(state_ref, forward_ref, wave_ref):
    rows, width, _ = state_ref.shape
    part = state_ref[...].reshape(rows * width, LANES)
    wave_ref[...] = dot(part, forward_ref[...]).astype(BF16).reshape(rows, width, 2 * LANES)


def tree_sum(terms):
    while len(terms) > 1:
        terms = [a + b for a, b in zip(terms[::2], terms[1::2])] + terms[len(terms) - len(terms) % 2:]
    return terms[0]


def product_kernel(first, rows_ref, wave_ref, mix_ref, after_ref, prod_ref, *rest):
    height, width, _ = wave_ref.shape
    if rest:
        rest[0][0:6] = wave_ref[0:6]
        rest[0][6:12] = wave_ref[height - 6:height]

    def channel_band(band, _):
        span = pl.ds(pl.multiple_of((band + first) * 16, 16), 16)
        target = pl.ds(pl.multiple_of(band * 16, 16), 16)
        weights = [mix_ref[tap, span] for tap in range(7)]

        def some_rows(index, _):
            for at in range(GROUP):
                spot = index * GROUP + at
                base = jnp.clip(rows_ref[1 + spot] - 3, 0, height - 7)
                terms = []
                for tap in range(7):
                    wave = wave_ref[base + tap, span]
                    terms.append(wave[:, :LANES] * weights[tap][:, :LANES])
                    terms.append(wave[:, LANES:] * weights[tap][:, LANES:])
                prod_ref[spot, target] = tree_sum(terms)
            return 0

        lax.fori_loop(0, MOST // GROUP, some_rows, 0)
        return 0

    lax.fori_loop(0, prod_ref.shape[1] // 16, channel_band, 0)


def block_kernel(last, block, rows_ref, flags_ref, state_ref, prod_one_ref, prod_two_ref, edge_wave_ref, row_even_ref, row_odd_ref,
                 column_even_ref, column_odd_ref, corner_even_ref, corner_odd_ref, own_even_ref, own_odd_ref,
                 mix_ref, side_ref, gain_ref, bias_ref, forward_ref, flipped_ref, inverse_ref, turn_ref, expand_ref,
                 reduce_ref, *rest):
    if last:
        out_ref, halo_ref, fix_ref, edge_ref, grid_ref, normed_ref, held_ref = rest
    else:
        (out_ref, send_row_even_ref, send_row_odd_ref, send_column_even_ref, send_column_odd_ref,
         halo_ref, fix_ref, edge_ref, grid_ref, normed_ref, low_ref, high_ref) = rest
    height, width, _ = state_ref.shape
    channels = 200
    pitch = height + 8
    count = rows_ref[0]
    even_row = flags_ref[0] == 0
    even_column = flags_ref[1] == 0
    fold = flags_ref[2] != 0

    def wave_of(rows, table):
        return dot(rows.reshape(3 * width, LANES), table).astype(BF16).reshape(3, width, 2 * LANES)

    left = jnp.where(even_column, column_odd_ref[...], column_even_ref[...])
    right = jnp.where(even_column, column_even_ref[...], column_odd_ref[...])
    low = jnp.where(even_column, own_odd_ref[...], own_even_ref[...])
    high = jnp.where(even_column, own_even_ref[...], own_odd_ref[...])
    grid_ref[0, 0:2] = left - high
    grid_ref[1, 0:2] = right - low
    halo_ref[0:3] = wave_of(jnp.where(even_row, row_odd_ref[...], row_even_ref[...]), forward_ref[...])
    for side in range(2):
        grid_ref[side, 2] = jnp.where(even_row, corner_odd_ref[side], corner_even_ref[side])

    @pl.when(jnp.logical_not(fold))
    def _():
        halo_ref[3:6] = wave_of(jnp.where(even_row, row_even_ref[...], row_odd_ref[...]), forward_ref[...])
        for side in range(2):
            grid_ref[side, 3] = jnp.where(even_row, corner_even_ref[side], corner_odd_ref[side])

    @pl.when(fold)
    def _():
        waves = wave_of(row_odd_ref[...], flipped_ref[...])
        for m in range(3):
            halo_ref[3 + m] = waves[2 - m]
        for side in range(2):
            grid_ref[side, 3] = dot(corner_odd_ref[1 - side], turn_ref[...]).astype(BF16)

    def corrections(index, _):
        span = pl.ds(pl.multiple_of(index * 16, 16), 16)
        lane = lane_ids((16, LANES))
        for side in range(2):
            totals = [jnp.where(lane % 4 == 3, bias_ref[side, span], 0.0)] * 2
            here, other = grid_ref[side, 0, span], grid_ref[side, 1, span]
            upward = jnp.where(lane < HALF, here, grid_ref[side, 3, span])
            downward = jnp.where(lane < HALF, grid_ref[side, 2, span], here)
            for tap_row in range(7):
                terms = [None, None]
                for tap in range(3):
                    shift = 4 * (tap_row - 3) + (tap if side == 0 else -tap)
                    weight = side_ref[(side * 7 + tap_row) * 3 + tap, span]

                    def moved(slab):
                        return pltpu.roll(slab, -shift % LANES, 1) if shift else slab

                    one, two = moved(here), moved(other)
                    if shift > 0:
                        first = jnp.where(lane < HALF, moved(upward), jnp.where(lane < LANES - shift, one, two))
                        second = jnp.where(lane < LANES - shift, two, one)
                    elif shift < 0:
                        first = jnp.where(lane >= HALF, moved(downward), jnp.where(lane >= -shift, one, two))
                        second = jnp.where(lane >= -shift, two, one)
                    else:
                        first, second = one, two
                    for group, value in enumerate((first, second)):
                        value = weight * value
                        terms[group] = value if terms[group] is None else terms[group] + value
                totals = [total + term.astype(F32) for total, term in zip(totals, terms)]
            for group in range(2):
                edge_ref[side, group, span] = totals[group].astype(BF16)
        return 0

    lax.fori_loop(0, width // 16, corrections, 0)

    def rim(band, _):
        span = pl.ds(pl.multiple_of(band * 16, 16), 16)
        weights = [mix_ref[tap, span] for tap in range(7)]
        for at in range(6):
            terms = []
            for tap in range(7):
                spot = (at if at < 3 else at - 3) + tap
                if at < 3:
                    wave = halo_ref[spot, span] if spot < 3 else edge_wave_ref[spot - 3, span]
                else:
                    wave = edge_wave_ref[6 + spot, span] if spot < 6 else halo_ref[spot - 3, span]
                terms.append(wave[:, :LANES] * weights[tap][:, :LANES])
                terms.append(wave[:, LANES:] * weights[tap][:, LANES:])
            fix_ref[at, span] = tree_sum(terms)
        return 0

    lax.fori_loop(0, width // 16, rim, 0)

    if last:
        held_ref[...] = jnp.zeros_like(held_ref)
    else:
        out_ref[...] = jnp.zeros_like(out_ref)
        low_ref[...] = jnp.zeros_like(low_ref)
        high_ref[...] = jnp.zeros_like(high_ref)

    def normalise(index, slot):
        lane = lane_ids((width, LANES))
        joined = []
        for at in range(GROUP):
            spot = GROUP * index + at
            row = rows_ref[1 + spot]
            place = (row + 16) % 64
            group = place // 32
            turn = lax.rem(LANES - 4 * (place % 32), LANES)
            left = pltpu.roll(edge_ref[0, group], turn, 1)
            right = pltpu.roll(edge_ref[1, group], lax.rem(turn + 4, LANES), 1)
            rim_row = (row < 3) | (row >= height - 3)
            fixed = fix_ref[jnp.clip(jnp.where(row < 3, row, row - (height - 6)), 0, 5)]
            prod = jnp.where(rim_row, fixed, jnp.concatenate([prod_one_ref[spot], prod_two_ref[spot]], axis=0))
            joined.append(jnp.concatenate([prod, jnp.where(lane < 4, left, right)], axis=1))
        depth = dot(jnp.concatenate(joined, axis=0), inverse_ref[...])
        for at in range(GROUP):
            real = depth[at * width:at * width + channels]
            center = jnp.mean(real, axis=0, keepdims=True)
            real = real - center
            spread = jnp.mean(real * real, axis=0, keepdims=True)
            normed = real * lax.rsqrt(spread + 1e-06) * gain_ref[0:channels]
            normed = jnp.concatenate([normed, jnp.ones((width - channels, LANES), F32)], axis=0).astype(BF16)
            normed_ref[slot, :, at * LANES:(at + 1) * LANES] = normed

    def pointwise(index, slot):
        half = dot(expand_ref[block], normed_ref[slot])
        half = half.astype(GELU)
        bend = jnp.tanh(half * (half * half * GELU(8.0 * 0.044715 * ROOT) + GELU(2.0 * ROOT)))
        hidden = (half + half * bend).astype(BF16)
        branch = dot(reduce_ref[block], hidden)
        for at in range(GROUP):
            row = rows_ref[1 + GROUP * index + at]
            value = branch[:, at * LANES:(at + 1) * LANES] + state_ref[row].astype(F32)
            if last:
                held_ref[pl.ds(row, channels, stride=pitch), :] = value[:channels]
            else:
                value = value.astype(BF16)
                out_ref[row] = value
                pack_edges(value, row, low_ref, high_ref)

    def mix(index, _):
        normalise(2 * index + 1, 1)
        pointwise(2 * index, 0)
        normalise(jnp.minimum(2 * index + 2, MOST // GROUP - 1), 0)
        pointwise(2 * index + 1, 1)
        return 0

    @pl.when(count > 0)
    def _():
        normalise(0, 0)
        lax.fori_loop(0, MOST // GROUP // 2, mix, 0)

    if last:
        def finish(index, _):
            out_ref[pl.ds(index * 8, 8)] = held_ref[pl.ds(index * 8 * pitch, 8 * pitch), :].reshape(8, pitch, LANES)[:, :height].astype(BF16)
            return 0

        lax.fori_loop(0, channels // 8, finish, 0)
    else:
        send_edges(flags_ref, out_ref, low_ref, high_ref, (send_row_even_ref, send_row_odd_ref),
                   (send_column_even_ref, send_column_odd_ref))


GELU = jnp.bfloat16
MOST = 48
EARLY = 7


def smem():
    return pl.BlockSpec(memory_space=pltpu.SMEM)


def vmem():
    return pl.BlockSpec(memory_space=pltpu.VMEM)


def shape(*dims, dtype=BF16):
    return jax.ShapeDtypeStruct(dims, dtype)


def params(mib):
    return pltpu.CompilerParams(vmem_limit_bytes=mib * 1024 * 1024)


def edge_shapes(width):
    return [shape(3, width, LANES), shape(3, width, LANES), shape(2, width, LANES), shape(2, width, LANES)]


def run_prepare(coef, table):
    blocks, width, _ = coef.shape
    one = [shape(7, width, 256), shape(42, width, LANES), shape(width, LANES, dtype=F32), shape(2, width, LANES, dtype=F32)]
    return pl.pallas_call(
        functools.partial(prepare_kernel, blocks),
        out_shape=one * blocks,
        in_specs=[vmem(), vmem()],
        out_specs=[vmem()] * (4 * blocks),
        compiler_params=params(24),
        cost_estimate=pl.CostEstimate(flops=2 * blocks * width * 160 * 7552, bytes_accessed=10_000_000, transcendentals=0),
        name="prepare",
    )(coef, table)


def run_stem(rows, flags, inverse, arrived, table, weight, height, width):
    return pl.pallas_call(
        stem_kernel,
        out_shape=[shape(height, width, LANES)] + edge_shapes(width),
        in_specs=[smem(), smem(), smem(), vmem(), vmem(), vmem()],
        out_specs=[vmem()] * 5,
        scratch_shapes=[
            pltpu.VMEM(arrived.shape, BF16),
            pltpu.VMEM((2, width, LANES), BF16),
            pltpu.VMEM((2, width, LANES), BF16),
        ],
        compiler_params=params(24),
        name="stem",
    )(rows, flags, inverse, arrived, table, weight)


def run_transform(state, forward):
    height, width, _ = state.shape
    return pl.pallas_call(
        transform_kernel,
        out_shape=shape(height, width, 2 * LANES),
        grid=(height // 16,),
        in_specs=[pl.BlockSpec((16, width, LANES), lambda i: (i, 0, 0)), pl.BlockSpec((LANES, 2 * LANES), lambda i: (0, 0))],
        out_specs=pl.BlockSpec((16, width, 2 * LANES), lambda i: (i, 0, 0)),
        compiler_params=params(24),
        cost_estimate=pl.CostEstimate(flops=2 * height * width * LANES * 256, bytes_accessed=10_000_000, transcendentals=0),
        name="transform",
    )(state, forward)


def run_product(rows, wave, mix, after, first, bands):
    _, width, _ = wave.shape
    edges = [shape(12, width, 2 * LANES)] if first else []
    return pl.pallas_call(
        functools.partial(product_kernel, first),
        out_shape=[shape(MOST, bands * 16, LANES)] + edges,
        in_specs=[smem(), vmem(), vmem(), pl.BlockSpec(memory_space=pl.ANY)],
        out_specs=[vmem()] * (1 + len(edges)),
        compiler_params=params(24),
        cost_estimate=pl.CostEstimate(flops=28 * MOST * bands * 16 * LANES, bytes_accessed=20_000_000, transcendentals=0),
        name="product",
    )(rows, wave, mix, after)


def corner_kernel(flags_ref, column_even_ref, column_odd_ref, own_even_ref, own_odd_ref, after_ref, corner_ref):
    even_column = flags_ref[1] == 0
    one = column_even_ref[0] - own_odd_ref[0]
    two = column_odd_ref[0] - own_even_ref[0]
    corner_ref[0] = jnp.where(even_column, two, one)
    corner_ref[1] = jnp.where(even_column, one, two)


def run_corner(flags, column_even, column_odd, own_even, own_odd, after):
    return pl.pallas_call(
        corner_kernel,
        out_shape=shape(*own_even.shape),
        in_specs=[smem()] + [vmem()] * 4 + [pl.BlockSpec(memory_space=pl.ANY)],
        out_specs=vmem(),
        compiler_params=params(16),
        cost_estimate=pl.CostEstimate(flops=1000, bytes_accessed=500_000, transcendentals=0),
        name="corner",
    )(flags, column_even, column_odd, own_even, own_odd, after)


def run_block(last, block, rows, flags, state, *arrays):
    height, width, _ = state.shape
    if last:
        out_shape = [shape(200, height, LANES)]
        extra = [pltpu.VMEM((200 * (height + 8), LANES), F32)]
    else:
        out_shape = [shape(height, width, LANES)] + edge_shapes(width)
        extra = [pltpu.VMEM((2, width, LANES), BF16)] * 2
    return pl.pallas_call(
        functools.partial(block_kernel, last, block),
        out_shape=out_shape,
        in_specs=[smem(), smem()] + [vmem()] * (1 + len(arrays)),
        out_specs=[vmem()] * len(out_shape),
        scratch_shapes=[
            pltpu.VMEM((6, width, 2 * LANES), BF16),
            pltpu.VMEM((6, width, LANES), BF16),
            pltpu.VMEM((2, 2, width, LANES), BF16),
            pltpu.VMEM((2, 4, width, LANES), BF16),
            pltpu.VMEM((2, width, GROUP * LANES), BF16),
        ] + extra,
        compiler_params=params(40),
        name="block",
    )(rows, flags, state, *arrays)


def wet_rows(wet):
    height = wet.shape[0]
    count = jnp.sum(wet)
    before = jnp.arange(height)[None, :] <= jnp.arange(height)[:, None]
    rank = jnp.sum(jnp.where(before, wet[None, :], 0), axis=1) - 1
    spot = jnp.minimum(jnp.arange(MOST), count - 1)
    hits = (rank[None, :] == spot[:, None]) & (wet[None, :] > 0)
    rows = jnp.sum(jnp.where(hits, jnp.arange(height)[None, :], 0), axis=1)
    return jnp.concatenate([count[None], rows]).astype(jnp.int32)


def split_high(value):
    high = value.astype(BF16)
    return high, value - high.astype(F32)


def coefficients(depth_weight, depth_bias, norm_gain, width):
    blocks, channels = depth_bias.shape
    taps, rest = split_high(depth_weight.reshape(blocks, channels, 49))
    gain_one, left = split_high(norm_gain[:, :, None])
    gain_two, left = split_high(left)
    bias_one, bias_left = split_high(depth_bias[:, :, None])
    parts = [taps, rest.astype(BF16), taps, gain_one, gain_two, left.astype(BF16), bias_one, bias_left.astype(BF16)]
    coef = jnp.concatenate(parts, axis=2)
    return jnp.pad(coef, ((0, 0), (0, width - channels), (0, 160 - coef.shape[2])))


def pointwise_weights(expand_weight, expand_bias, reduce_weight, width):
    blocks, channels, hidden = expand_weight.shape
    spare = width - channels
    high, low = split_high(0.5 * expand_bias[:, None, :])
    expand = jnp.concatenate(
        [expand_weight * BF16(0.5), high, low.astype(BF16), jnp.zeros((blocks, spare - 2, hidden), BF16)], axis=1
    )
    reduce = jnp.pad(reduce_weight, ((0, 0), (0, 0), (0, spare)))
    return jnp.transpose(expand, (0, 2, 1)), jnp.transpose(reduce, (0, 2, 1))


def body(
    atm_flux,
    owner_map,
    wet_mask,
    stem_weight,
    depth_weight,
    depth_bias,
    norm_gain,
    expand_weight,
    expand_bias,
    reduce_weight,
):
    lon_count = lax.axis_size("gx")
    lat_count = lax.axis_size("gy")
    lon_index = lax.axis_index("gx")
    lat_index = lax.axis_index("gy")
    blocks, channels = depth_bias.shape
    width = (channels + 15) // 16 * 16
    height = wet_mask.shape[0]
    arrived = lax.all_to_all(atm_flux[0], ("gx", "gy"), split_axis=0, concat_axis=0, tiled=True)[:, 0]
    pieces = owner_map.shape[0]
    owner = owner_map[:, 0]
    inverse = jnp.sum(
        jnp.where(owner[None, :] == jnp.arange(pieces)[:, None], jnp.arange(pieces)[None, :], 0), axis=1
    ).astype(jnp.int32)
    rows = wet_rows(wet_mask[:, 0])
    flags = jnp.stack([lat_index % 2, lon_index % 2, lat_index == lat_count - 1]).astype(jnp.int32)
    stem = jnp.transpose(stem_weight, (0, 2, 3, 1)).reshape(channels, -1)
    stem = jnp.pad(stem, ((0, width - channels), (0, 0)))
    forward, back = fourier_tables()
    flipped = jnp.asarray(forward[::-1], BF16)
    forward = jnp.asarray(forward, BF16)
    back = jnp.asarray(back, BF16)
    turn = jnp.asarray(fold_table(), BF16)
    coef = coefficients(depth_weight, depth_bias, norm_gain, width)
    prepared = run_prepare(coef, jnp.asarray(prepare_table(), BF16))
    expand, reduce = pointwise_weights(expand_weight, expand_bias, reduce_weight, width)
    arrived, prepared, expand, reduce = lax.optimization_barrier((arrived, prepared, expand, reduce))
    state, *edges = run_stem(
        rows, flags, inverse, arrived, jnp.asarray(deinterleave_table(), BF16), stem, height, width
    )
    lon_even = [(i, i ^ 1) for i in range(lon_count)]
    lon_odd = [(i, ((i - 1 ^ 1) + 1) % lon_count) for i in range(lon_count)]
    lat_even = [(i, i ^ 1) for i in range(lat_count)]
    top = lat_count - 1
    lat_odd = []
    for lon in range(lon_count):
        for lat in range(1, top):
            lat_odd.append((lon * lat_count + lat, lon * lat_count + (lat - 1 ^ 1) + 1))
        lat_odd.append((lon * lat_count + top, (lon_count - 1 - lon) * lat_count + top))
    for index in range(blocks):
        last = index == blocks - 1
        row_even, row_odd, own_even, own_odd = edges
        column_even = lax.ppermute(own_even, "gx", lon_even)
        column_odd = lax.ppermute(own_odd, "gx", lon_odd)
        row_even = lax.ppermute(row_even, "gy", lat_even)
        row_odd = lax.ppermute(row_odd, ("gx", "gy"), lat_odd)
        mix, side, gain, bias = prepared[4 * index:4 * index + 4]
        bands = width // 16
        wave = run_transform(state, forward)
        prod = run_product(rows, wave, mix, wave, 0, EARLY)
        corner = run_corner(flags, column_even, column_odd, own_even, own_odd, prod[0])
        corner_even = lax.ppermute(corner, "gy", lat_even)
        corner_odd = lax.ppermute(corner, ("gx", "gy"), lat_odd)
        prod += run_product(rows, wave, mix, corner, EARLY, bands - EARLY)
        out = run_block(
            last, index, rows, flags, state, *prod, row_even, row_odd, column_even, column_odd,
            corner_even, corner_odd, own_even, own_odd, mix, side, gain, bias, forward, flipped, back, turn,
            expand, reduce,
        )
        if last:
            return out[0]
        state, *edges = out


def solution(mesh):
    return jax.shard_map(
        body,
        mesh=mesh,
        in_specs=(
            P(("gx", "gy"), None, None, None, None),
            P(None, ("gx", "gy")),
            P("gy", "gx"),
            P(),
            P(),
            P(),
            P(),
            P(),
            P(),
            P(),
        ),
        out_specs=P(None, "gy", "gx"),
        check_vma=False,
    )
```

```python
import functools

import jax
import jax.numpy as jnp
import numpy as np
from jax import lax
from jax.experimental import pallas as pl
from jax.experimental.pallas import tpu as pltpu
from jax.sharding import PartitionSpec as P

LANES = 128
GROUP = 8
HALF = LANES // 2
ROOT = float(np.sqrt(2.0 / np.pi))
BF16 = jnp.bfloat16
F32 = jnp.float32


def fourier_tables():
    spot = np.arange(LANES)[:, None]
    wave = np.arange(HALF)[None, :]
    angle = 2.0 * np.pi * (spot * wave % LANES) / LANES
    cos, sin = np.cos(angle), np.sin(angle)
    plain = np.concatenate([cos, -sin], axis=1)
    plain[:, HALF] = np.where(np.arange(LANES) % 2 == 0, 1.0, -1.0)
    swapped = np.concatenate([-sin, cos], axis=1)
    swapped[:, 0] = 0.0
    swapped[:, HALF] = 0.0
    forward = np.concatenate([plain, swapped], axis=1)
    inverse = plain.T * (2.0 / LANES)
    inverse[0] /= 2.0
    inverse[HALF] /= 2.0
    edges = np.zeros((LANES, LANES))
    for j in range(3):
        edges[j, j] = 1.0
        edges[4 + j, LANES - 3 + j] = 1.0
    edges[3, :] = 1.0
    edges[7, :] = 1.0
    inverse = np.concatenate([inverse, edges], axis=0)
    return forward, inverse


def fold_table():
    table = np.zeros((LANES, LANES))
    spot = np.arange(LANES - 1)
    table[LANES - 2 - spot, spot] = 1.0
    return table


def dot(left, right):
    return jnp.dot(left, right, preferred_element_type=F32)


def lane_ids(shape):
    return lax.broadcasted_iota(jnp.int32, shape, len(shape) - 1)


def pack_edges(value, row, low_ref, high_ref):
    place = (row + 16) % 64
    group = place // 32
    start = 4 * (place % 32)
    lane = lane_ids(value.shape)
    hit = (lane >= start) & (lane < start + 3)
    low = pltpu.roll(value, start, 1)
    high = pltpu.roll(value, lax.rem(start + 3, LANES), 1)
    low_ref[group] = jnp.where(hit, low, low_ref[group])
    high_ref[group] = jnp.where(hit, high, high_ref[group])


def send_edges(flags_ref, state_ref, low_ref, high_ref, row_refs, column_refs):
    height = state_ref.shape[0]
    even_row = flags_ref[0] == 0
    even_column = flags_ref[1] == 0
    row_refs[0][...] = state_ref[pl.ds(jnp.where(even_row, height - 3, 0), 3)]
    row_refs[1][...] = state_ref[pl.ds(jnp.where(even_row, 0, height - 3), 3)]
    column_refs[0][...] = jnp.where(even_column, high_ref[...], low_ref[...])
    column_refs[1][...] = jnp.where(even_column, low_ref[...], high_ref[...])


def prepare_kernel(blocks, coef_ref, table_ref, stem_ref, *outs):
    outs[-1][...] = stem_ref[...]
    spot = lax.broadcasted_iota(jnp.int32, (coef_ref.shape[2], LANES), 0)
    phase = lane_ids((coef_ref.shape[2], LANES)) % 4
    for block in range(blocks):
        mix_ref, side_ref, gain_ref, bias_ref = outs[4 * block:4 * block + 4]
        coef = coef_ref[block]
        for tap in range(7):
            mix_ref[tap] = dot(coef, table_ref[:, tap * 256:(tap + 1) * 256]).astype(BF16)
        for pair in range(21):
            tables = []
            for entry in (2 * pair, 2 * pair + 1):
                side, row, tap = entry // 21, entry % 21 // 3, entry % 3
                source = row * 7 + (tap if side == 0 else 6 - tap)
                inside = phase <= 2 - tap if side == 0 else (phase >= tap) & (phase <= 2)
                tables.append(jnp.where(((spot == source) | (spot == source + 49)) & inside, 1.0, 0.0).astype(BF16))
            out = dot(coef, jnp.concatenate(tables, axis=1)).astype(BF16)
            side_ref[2 * pair] = out[:, :LANES]
            side_ref[2 * pair + 1] = out[:, LANES:]
        out = dot(coef, table_ref[:, 1792:2176])
        gain_ref[...] = out[:, :LANES]
        bias_ref[0] = out[:, LANES:2 * LANES]
        bias_ref[1] = out[:, 2 * LANES:]


def prepare_table():
    table = np.zeros((160, 2176))
    angle = 2.0 * np.pi * np.arange(HALF + 1)[None, :] * (np.arange(7)[:, None] - 3) / LANES
    cos, sin = np.cos(angle), np.sin(angle)
    none = np.zeros((7, 1))
    real = np.concatenate([cos, cos[:, 1:HALF]], axis=1)
    imag = np.concatenate([none, -sin[:, 1:HALF], none, sin[:, 1:HALF]], axis=1)
    wave = np.concatenate([real, imag], axis=1)
    wave_high = wave.astype(BF16).astype(np.float64)
    for row in range(7):
        for tap in range(7):
            spot = row * 7 + tap
            table[spot, row * 256:(row + 1) * 256] = wave_high[tap]
            table[49 + spot, row * 256:(row + 1) * 256] = wave_high[tap]
            table[98 + spot, row * 256:(row + 1) * 256] = wave[tap] - wave_high[tap]
    table[147:150, 1792:1920] = 1.0
    table[150, 1920:2048] = 1.0
    table[151, 2048:2176] = 1.0
    return table


def stem_kernel(rows_ref, flags_ref, owner_ref, arrived_ref, weight_ref, state_ref, row_even_ref, row_odd_ref,
                column_even_ref, column_odd_ref, inverse_ref, split_ref, low_ref, high_ref):
    pieces = arrived_ref.shape[0]
    flux = arrived_ref.shape[1]
    step = 32

    def invert(index, _):
        for at in range(8):
            inverse_ref[owner_ref[index * 8 + at]] = index * 8 + at
        return 0

    lax.fori_loop(0, pieces // 8, invert, 0)
    source = lax.broadcasted_iota(jnp.int32, (2 * LANES, 2 * LANES), 0)
    target = lane_ids((2 * LANES, 2 * LANES))
    wanted = jnp.where(target < LANES, 2 * target, 2 * target - (2 * LANES - 1))
    table = jnp.where(source == wanted, 1.0, 0.0).astype(BF16)

    def split(index, _):
        part = arrived_ref[pl.ds(index * step, step)].reshape(step * flux, 2 * LANES)
        split_ref[pl.ds(index * step, step)] = dot(part, table).astype(BF16).reshape(step, flux, 2 * LANES)
        return 0

    lax.fori_loop(0, pieces // step, split, 0)
    state_ref[...] = jnp.zeros_like(state_ref)
    low_ref[...] = jnp.zeros_like(low_ref)
    high_ref[...] = jnp.zeros_like(high_ref)

    def group(index, _):
        rows = [rows_ref[1 + GROUP * index + at] for at in range(GROUP)]
        columns = []
        for row in rows:
            one = split_ref[inverse_ref[2 * row]]
            two = split_ref[inverse_ref[2 * row + 1]]
            columns.append(jnp.concatenate([one[:, :LANES], one[:, LANES:], two[:, :LANES], two[:, LANES:]], axis=0))
        out = dot(weight_ref[...], jnp.concatenate(columns, axis=1))
        for at, row in enumerate(rows):
            value = out[:, at * LANES:(at + 1) * LANES].astype(BF16)
            state_ref[row] = value
            pack_edges(value, row, low_ref, high_ref)
        return 0

    @pl.when(rows_ref[0] > 0)
    def _():
        lax.fori_loop(0, MOST // GROUP, group, 0)

    send_edges(flags_ref, state_ref, low_ref, high_ref, (row_even_ref, row_odd_ref), (column_even_ref, column_odd_ref))


def transform_kernel(state_ref, forward_ref, wave_ref):
    rows, width, _ = state_ref.shape
    part = state_ref[...].reshape(rows * width, LANES)
    wave_ref[...] = dot(part, forward_ref[...]).astype(BF16).reshape(rows, width, 2 * LANES)


def tree_sum(terms):
    while len(terms) > 1:
        terms = [a + b for a, b in zip(terms[::2], terms[1::2])] + terms[len(terms) - len(terms) % 2:]
    return terms[0]


def product_kernel(first, rows_ref, wave_ref, mix_ref, after_ref, prod_ref, *rest):
    height, width, _ = wave_ref.shape
    if rest:
        rest[0][0:6] = wave_ref[0:6]
        rest[0][6:12] = wave_ref[height - 6:height]

    def channel_band(band, _):
        span = pl.ds(pl.multiple_of((band + first) * 16, 16), 16)
        target = pl.ds(pl.multiple_of(band * 16, 16), 16)
        weights = [mix_ref[tap, span] for tap in range(7)]

        def some_rows(index, _):
            for at in range(GROUP):
                spot = index * GROUP + at
                base = jnp.clip(rows_ref[1 + spot] - 3, 0, height - 7)
                terms = []
                for tap in range(7):
                    wave = wave_ref[base + tap, span]
                    terms.append(wave[:, :LANES] * weights[tap][:, :LANES])
                    terms.append(wave[:, LANES:] * weights[tap][:, LANES:])
                prod_ref[spot, target] = tree_sum(terms)
            return 0

        lax.fori_loop(0, MOST // GROUP, some_rows, 0)
        return 0

    lax.fori_loop(0, prod_ref.shape[1] // 16, channel_band, 0)


def block_kernel(last, block, rows_ref, flags_ref, state_ref, prod_one_ref, prod_two_ref, edge_wave_ref, row_even_ref, row_odd_ref,
                 column_even_ref, column_odd_ref, own_even_ref, own_odd_ref, mix_ref, side_ref, gain_ref,
                 bias_ref, forward_ref, flipped_ref, inverse_ref, turn_ref, expand_ref, reduce_ref, *rest):
    if last:
        out_ref, halo_ref, fix_ref, edge_ref, grid_ref, normed_ref, held_ref = rest
    else:
        (out_ref, send_row_even_ref, send_row_odd_ref, send_column_even_ref, send_column_odd_ref,
         halo_ref, fix_ref, edge_ref, grid_ref, normed_ref, low_ref, high_ref) = rest
    height, width, _ = state_ref.shape
    channels = 200
    pitch = height + 8
    count = rows_ref[0]
    even_row = flags_ref[0] == 0
    even_column = flags_ref[1] == 0
    fold = flags_ref[2] != 0

    def wave_of(rows, table):
        return dot(rows.reshape(3 * width, LANES), table).astype(BF16).reshape(3, width, 2 * LANES)

    left = jnp.where(even_column, column_odd_ref[...], column_even_ref[...])
    right = jnp.where(even_column, column_even_ref[...], column_odd_ref[...])
    low = jnp.where(even_column, own_odd_ref[...], own_even_ref[...])
    high = jnp.where(even_column, own_even_ref[...], own_odd_ref[...])
    grid_ref[0, 0:2] = left - high
    grid_ref[1, 0:2] = right - low
    halo_ref[0:3] = wave_of(jnp.where(even_row, row_odd_ref[0:3], row_even_ref[0:3]), forward_ref[...])
    for side in range(2):
        grid_ref[side, 2] = jnp.where(even_row, row_odd_ref[3 + side], row_even_ref[3 + side])

    @pl.when(jnp.logical_not(fold))
    def _():
        halo_ref[3:6] = wave_of(jnp.where(even_row, row_even_ref[0:3], row_odd_ref[0:3]), forward_ref[...])
        for side in range(2):
            grid_ref[side, 3] = jnp.where(even_row, row_even_ref[3 + side], row_odd_ref[3 + side])

    @pl.when(fold)
    def _():
        waves = wave_of(row_odd_ref[0:3], flipped_ref[...])
        for m in range(3):
            halo_ref[3 + m] = waves[2 - m]
        for side in range(2):
            grid_ref[side, 3] = dot(row_odd_ref[4 - side], turn_ref[...]).astype(BF16)

    def corrections(index, _):
        span = pl.ds(pl.multiple_of(index * 16, 16), 16)
        lane = lane_ids((16, LANES))
        for side in range(2):
            totals = [jnp.where(lane % 4 == 3, bias_ref[side, span], 0.0)] * 2
            here, other = grid_ref[side, 0, span], grid_ref[side, 1, span]
            upward = jnp.where(lane < HALF, here, grid_ref[side, 3, span])
            downward = jnp.where(lane < HALF, grid_ref[side, 2, span], here)
            slabs = [here, other, upward, downward]
            turned = [[pltpu.roll(slab, (-tap if side == 0 else tap) % LANES, 1) if tap else slab for tap in range(3)]
                      for slab in slabs]
            for tap_row in range(7):
                shift = 4 * (tap_row - 3)
                weights = [side_ref[(side * 7 + tap_row) * 3 + tap, span] for tap in range(3)]

                def moved(at):
                    value = weights[0] * turned[at][0] + weights[1] * turned[at][1] + weights[2] * turned[at][2]
                    return pltpu.roll(value, -shift % LANES, 1) if shift else value

                first, second = moved(0), moved(1)
                if shift > 0:
                    inner = lane < LANES - shift
                    first, second = jnp.where(inner, first, second), jnp.where(inner, second, first)
                    first = jnp.where((lane < HALF) & (lane >= HALF - shift), moved(2), first)
                elif shift < 0:
                    inner = lane >= -shift
                    first, second = jnp.where(inner, first, second), jnp.where(inner, second, first)
                    first = jnp.where((lane >= HALF) & (lane < HALF - shift), moved(3), first)
                totals = [totals[0] + first.astype(F32), totals[1] + second.astype(F32)]
            for group in range(2):
                edge_ref[side, group, span] = totals[group].astype(BF16)
        return 0

    lax.fori_loop(0, width // 16, corrections, 0)

    def rim(band, _):
        span = pl.ds(pl.multiple_of(band * 16, 16), 16)
        weights = [mix_ref[tap, span] for tap in range(7)]
        for at in range(6):
            terms = []
            for tap in range(7):
                spot = (at if at < 3 else at - 3) + tap
                if at < 3:
                    wave = halo_ref[spot, span] if spot < 3 else edge_wave_ref[spot - 3, span]
                else:
                    wave = edge_wave_ref[6 + spot, span] if spot < 6 else halo_ref[spot - 3, span]
                terms.append(wave[:, :LANES] * weights[tap][:, :LANES])
                terms.append(wave[:, LANES:] * weights[tap][:, LANES:])
            fix_ref[at, span] = tree_sum(terms)
        return 0

    lax.fori_loop(0, width // 16, rim, 0)

    if last:
        held_ref[...] = jnp.zeros_like(held_ref)
    else:
        out_ref[...] = jnp.zeros_like(out_ref)
        low_ref[...] = jnp.zeros_like(low_ref)
        high_ref[...] = jnp.zeros_like(high_ref)

    def normalise(index, slot):
        lane = lane_ids((width, LANES))
        joined = []
        for at in range(GROUP):
            spot = GROUP * index + at
            row = rows_ref[1 + spot]
            place = (row + 16) % 64
            group = place // 32
            turn = lax.rem(LANES - 4 * (place % 32), LANES)
            left = pltpu.roll(edge_ref[0, group], turn, 1)
            right = pltpu.roll(edge_ref[1, group], lax.rem(turn + 4, LANES), 1)
            rim_row = (row < 3) | (row >= height - 3)
            fixed = fix_ref[jnp.clip(jnp.where(row < 3, row, row - (height - 6)), 0, 5)]
            prod = jnp.where(rim_row, fixed, jnp.concatenate([prod_one_ref[spot], prod_two_ref[spot]], axis=0))
            joined.append(jnp.concatenate([prod, jnp.where(lane < 4, left, right)], axis=1))
        depth = dot(jnp.concatenate(joined, axis=0), inverse_ref[...])
        for at in range(GROUP):
            real = depth[at * width:at * width + channels]
            center = jnp.mean(real, axis=0, keepdims=True)
            real = real - center
            spread = jnp.mean(real * real, axis=0, keepdims=True)
            normed = real * lax.rsqrt(spread + 1e-06) * gain_ref[0:channels]
            normed = jnp.concatenate([normed, jnp.ones((width - channels, LANES), F32)], axis=0).astype(BF16)
            normed_ref[slot, :, at * LANES:(at + 1) * LANES] = normed

    def pointwise(index, slot):
        half = dot(expand_ref[block], normed_ref[slot])
        half = half.astype(GELU)
        bend = jnp.tanh(half * (half * half * GELU(8.0 * 0.044715 * ROOT) + GELU(2.0 * ROOT)))
        hidden = (half + half * bend).astype(BF16)
        branch = dot(reduce_ref[block], hidden)
        for at in range(GROUP):
            row = rows_ref[1 + GROUP * index + at]
            value = branch[:, at * LANES:(at + 1) * LANES] + state_ref[row].astype(F32)[:channels]
            if last:
                held_ref[pl.ds(row, channels, stride=pitch), :] = value
            else:
                value = jnp.concatenate([value, jnp.zeros((width - channels, LANES), F32)], axis=0).astype(BF16)
                out_ref[row] = value
                pack_edges(value, row, low_ref, high_ref)

    @pl.when(count > 0)
    def _():
        groups = MOST // GROUP
        normalise(0, 0)
        for index in range(groups):
            if index < groups - 1:
                normalise(index + 1, (index + 1) % 2)
            pointwise(index, index % 2)

    if last:
        def finish(index, _):
            out_ref[pl.ds(index * 8, 8)] = held_ref[pl.ds(index * 8 * pitch, 8 * pitch), :].reshape(8, pitch, LANES)[:, :height].astype(BF16)
            return 0

        lax.fori_loop(0, channels // 8, finish, 0)
    else:
        send_edges(flags_ref, out_ref, low_ref, high_ref, (send_row_even_ref, send_row_odd_ref),
                   (send_column_even_ref, send_column_odd_ref))


GELU = jnp.bfloat16
MOST = 48
EARLY = 4


def smem():
    return pl.BlockSpec(memory_space=pltpu.SMEM)


def vmem():
    return pl.BlockSpec(memory_space=pltpu.VMEM)


def shape(*dims, dtype=BF16):
    return jax.ShapeDtypeStruct(dims, dtype)


def params(mib):
    return pltpu.CompilerParams(vmem_limit_bytes=mib * 1024 * 1024)


def edge_shapes(width):
    return [shape(3, width, LANES), shape(3, width, LANES), shape(2, width, LANES), shape(2, width, LANES)]


def run_prepare(coef, table, stem):
    blocks, width, _ = coef.shape
    one = [shape(7, width, 256), shape(42, width, LANES), shape(width, LANES, dtype=F32), shape(2, width, LANES, dtype=F32)]
    return pl.pallas_call(
        functools.partial(prepare_kernel, blocks),
        out_shape=one * blocks + [shape(*stem.shape)],
        in_specs=[vmem()] * 3,
        out_specs=[vmem()] * (4 * blocks + 1),
        compiler_params=params(16),
        cost_estimate=pl.CostEstimate(flops=2 * blocks * width * 160 * 7552, bytes_accessed=10_000_000, transcendentals=0),
        name="prepare",
    )(coef, table, stem)


def run_stem(rows, flags, owner, arrived, weight, height, width):
    return pl.pallas_call(
        stem_kernel,
        out_shape=[shape(height, width, LANES)] + edge_shapes(width),
        in_specs=[smem(), smem(), smem(), vmem(), vmem()],
        out_specs=[vmem()] * 5,
        scratch_shapes=[
            pltpu.SMEM(owner.shape, jnp.int32),
            pltpu.VMEM(arrived.shape, BF16),
            pltpu.VMEM((2, width, LANES), BF16),
            pltpu.VMEM((2, width, LANES), BF16),
        ],
        compiler_params=params(24),
        name="stem",
    )(rows, flags, owner, arrived, weight)


def run_transform(state, forward):
    height, width, _ = state.shape
    return pl.pallas_call(
        transform_kernel,
        out_shape=shape(height, width, 2 * LANES),
        grid=(height // 16,),
        in_specs=[pl.BlockSpec((16, width, LANES), lambda i: (i, 0, 0)), pl.BlockSpec((LANES, 2 * LANES), lambda i: (0, 0))],
        out_specs=pl.BlockSpec((16, width, 2 * LANES), lambda i: (i, 0, 0)),
        compiler_params=params(24),
        cost_estimate=pl.CostEstimate(flops=2 * height * width * LANES * 256, bytes_accessed=10_000_000, transcendentals=0),
        name="transform",
    )(state, forward)


def run_product(rows, wave, mix, after, first, bands):
    _, width, _ = wave.shape
    edges = [shape(12, width, 2 * LANES)] if first else []
    return pl.pallas_call(
        functools.partial(product_kernel, first),
        out_shape=[shape(MOST, bands * 16, LANES)] + edges,
        in_specs=[smem(), vmem(), vmem(), pl.BlockSpec(memory_space=pl.ANY)],
        out_specs=[vmem()] * (1 + len(edges)),
        compiler_params=params(24),
        cost_estimate=pl.CostEstimate(flops=28 * MOST * bands * 16 * LANES, bytes_accessed=20_000_000, transcendentals=0),
        name="product",
    )(rows, wave, mix, after)


def corner_kernel(flags_ref, column_even_ref, column_odd_ref, own_even_ref, own_odd_ref, strip_even_ref, strip_odd_ref,
                  after_ref, row_even_ref, row_odd_ref):
    even_column = flags_ref[1] == 0
    one = column_even_ref[0] - own_odd_ref[0]
    two = column_odd_ref[0] - own_even_ref[0]
    for strip_ref, row_ref in ((strip_even_ref, row_even_ref), (strip_odd_ref, row_odd_ref)):
        row_ref[0:3] = strip_ref[...]
        row_ref[3] = jnp.where(even_column, two, one)
        row_ref[4] = jnp.where(even_column, one, two)


def run_corner(flags, column_even, column_odd, own_even, own_odd, strip_even, strip_odd, after):
    _, width, _ = own_even.shape
    return pl.pallas_call(
        corner_kernel,
        out_shape=[shape(5, width, LANES)] * 2,
        in_specs=[smem()] + [vmem()] * 6 + [pl.BlockSpec(memory_space=pl.ANY)],
        out_specs=[vmem()] * 2,
        compiler_params=params(16),
        cost_estimate=pl.CostEstimate(flops=1000, bytes_accessed=500_000, transcendentals=0),
        name="corner",
    )(flags, column_even, column_odd, own_even, own_odd, strip_even, strip_odd, after)


def run_block(last, block, rows, flags, state, *arrays):
    height, width, _ = state.shape
    if last:
        out_shape = [shape(200, height, LANES)]
        extra = [pltpu.VMEM((200 * (height + 8), LANES), F32)]
    else:
        out_shape = [shape(height, width, LANES)] + edge_shapes(width)
        extra = [pltpu.VMEM((2, width, LANES), BF16)] * 2
    return pl.pallas_call(
        functools.partial(block_kernel, last, block),
        out_shape=out_shape,
        in_specs=[smem(), smem()] + [vmem()] * (1 + len(arrays)),
        out_specs=[vmem()] * len(out_shape),
        scratch_shapes=[
            pltpu.VMEM((6, width, 2 * LANES), BF16),
            pltpu.VMEM((6, width, LANES), BF16),
            pltpu.VMEM((2, 2, width, LANES), BF16),
            pltpu.VMEM((2, 4, width, LANES), BF16),
            pltpu.VMEM((2, width, GROUP * LANES), BF16),
        ] + extra,
        compiler_params=params(28),
        name="block",
    )(rows, flags, state, *arrays)


def wet_rows(wet):
    height = wet.shape[0]
    count = jnp.sum(wet)
    before = jnp.arange(height)[None, :] <= jnp.arange(height)[:, None]
    rank = jnp.sum(jnp.where(before, wet[None, :], 0), axis=1) - 1
    spot = jnp.minimum(jnp.arange(MOST), count - 1)
    hits = (rank[None, :] == spot[:, None]) & (wet[None, :] > 0)
    rows = jnp.sum(jnp.where(hits, jnp.arange(height)[None, :], 0), axis=1)
    return jnp.concatenate([count[None], rows]).astype(jnp.int32)


def split_high(value):
    high = value.astype(BF16)
    return high, value - high.astype(F32)


def coefficients(depth_weight, depth_bias, norm_gain, width):
    blocks, channels = depth_bias.shape
    taps, rest = split_high(depth_weight.reshape(blocks, channels, 49))
    gain_one, left = split_high(norm_gain[:, :, None])
    gain_two, left = split_high(left)
    bias_one, bias_left = split_high(depth_bias[:, :, None])
    parts = [taps, rest.astype(BF16), taps, gain_one, gain_two, left.astype(BF16), bias_one, bias_left.astype(BF16)]
    coef = jnp.concatenate(parts, axis=2)
    return jnp.pad(coef, ((0, 0), (0, width - channels), (0, 160 - coef.shape[2])))


def pointwise_weights(expand_weight, expand_bias, reduce_weight, width):
    blocks, channels, hidden = expand_weight.shape
    spare = width - channels
    high, low = split_high(0.5 * expand_bias[:, None, :])
    expand = jnp.concatenate(
        [expand_weight * BF16(0.5), high, low.astype(BF16), jnp.zeros((blocks, spare - 2, hidden), BF16)], axis=1
    )
    return jnp.transpose(lax.optimization_barrier(expand), (0, 2, 1)), jnp.transpose(reduce_weight, (0, 2, 1))


def body(
    atm_flux,
    owner_map,
    wet_mask,
    stem_weight,
    depth_weight,
    depth_bias,
    norm_gain,
    expand_weight,
    expand_bias,
    reduce_weight,
):
    lon_count = lax.axis_size("gx")
    lat_count = lax.axis_size("gy")
    lon_index = lax.axis_index("gx")
    lat_index = lax.axis_index("gy")
    blocks, channels = depth_bias.shape
    width = (channels + 15) // 16 * 16
    height = wet_mask.shape[0]
    arrived = lax.all_to_all(atm_flux[0], ("gx", "gy"), split_axis=0, concat_axis=0, tiled=True)[:, 0]
    owner = owner_map[:, 0]
    rows = wet_rows(wet_mask[:, 0])
    flags = jnp.stack([lat_index % 2, lon_index % 2, lat_index == lat_count - 1]).astype(jnp.int32)
    stem = jnp.transpose(stem_weight, (0, 2, 3, 1)).reshape(channels, -1)
    stem = jnp.pad(stem, ((0, width - channels), (0, 0)))
    forward, back = fourier_tables()
    flipped = jnp.asarray(forward[::-1], BF16)
    forward = jnp.asarray(forward, BF16)
    back = jnp.asarray(back, BF16)
    turn = jnp.asarray(fold_table(), BF16)
    coef = coefficients(depth_weight, depth_bias, norm_gain, width)
    prepared = run_prepare(coef, jnp.asarray(prepare_table(), BF16), stem)
    expand, reduce = pointwise_weights(expand_weight, expand_bias, reduce_weight, width)
    arrived, prepared, expand, reduce = lax.optimization_barrier((arrived, prepared, expand, reduce))
    state, *edges = run_stem(rows, flags, owner, arrived, prepared[-1], height, width)
    lon_even = [(i, i ^ 1) for i in range(lon_count)]
    lon_odd = [(i, ((i - 1 ^ 1) + 1) % lon_count) for i in range(lon_count)]
    lat_even = [(i, i ^ 1) for i in range(lat_count)]
    top = lat_count - 1
    lat_odd = []
    for lon in range(lon_count):
        for lat in range(1, top):
            lat_odd.append((lon * lat_count + lat, lon * lat_count + (lat - 1 ^ 1) + 1))
        lat_odd.append((lon * lat_count + top, (lon_count - 1 - lon) * lat_count + top))
    for index in range(blocks):
        last = index == blocks - 1
        row_even, row_odd, own_even, own_odd = edges
        column_even = lax.ppermute(own_even, "gx", lon_even)
        column_odd = lax.ppermute(own_odd, "gx", lon_odd)
        mix, side, gain, bias = prepared[4 * index:4 * index + 4]
        bands = width // 16
        wave = run_transform(state, forward)
        prod = run_product(rows, wave, mix, wave, 0, EARLY)
        row_even, row_odd = run_corner(flags, column_even, column_odd, own_even, own_odd, row_even, row_odd, prod[0])
        prod += run_product(rows, wave, mix, row_odd, EARLY, bands - EARLY)
        row_even = lax.ppermute(row_even, "gy", lat_even)
        row_odd = lax.ppermute(row_odd, ("gx", "gy"), lat_odd)
        out = run_block(
            last, index, rows, flags, state, *prod, row_even, row_odd, column_even, column_odd,
            own_even, own_odd, mix, side, gain, bias, forward, flipped, back, turn,
            expand, reduce,
        )
        if last:
            return out[0]
        state, *edges = out


def solution(mesh):
    return jax.shard_map(
        body,
        mesh=mesh,
        in_specs=(
            P(("gx", "gy"), None, None, None, None),
            P(None, ("gx", "gy")),
            P("gy", "gx"),
            P(),
            P(),
            P(),
            P(),
            P(),
            P(),
            P(),
        ),
        out_specs=P(None, "gy", "gx"),
        check_vma=False,
    )
```

```python
import functools

import jax
import jax.numpy as jnp
import numpy as np
from jax import lax
from jax.experimental import pallas as pl
from jax.experimental.pallas import tpu as pltpu
from jax.sharding import PartitionSpec as P

LANES = 128
GROUP = 8
HALF = LANES // 2
ROOT = float(np.sqrt(2.0 / np.pi))
BF16 = jnp.bfloat16
F32 = jnp.float32


def fourier_tables():
    spot = np.arange(LANES)[:, None]
    wave = np.arange(HALF)[None, :]
    angle = 2.0 * np.pi * (spot * wave % LANES) / LANES
    cos, sin = np.cos(angle), np.sin(angle)
    plain = np.concatenate([cos, -sin], axis=1)
    plain[:, HALF] = np.where(np.arange(LANES) % 2 == 0, 1.0, -1.0)
    swapped = np.concatenate([-sin, cos], axis=1)
    swapped[:, 0] = 0.0
    swapped[:, HALF] = 0.0
    forward = np.concatenate([plain, swapped], axis=1)
    inverse = plain.T * (2.0 / LANES)
    inverse[0] /= 2.0
    inverse[HALF] /= 2.0
    edges = np.zeros((LANES, LANES))
    for j in range(3):
        edges[j, j] = 1.0
        edges[4 + j, LANES - 3 + j] = 1.0
    edges[3, :] = 1.0
    edges[7, :] = 1.0
    inverse = np.concatenate([inverse, edges], axis=0)
    return forward, inverse


def fold_table():
    table = np.zeros((LANES, LANES))
    spot = np.arange(LANES - 1)
    table[LANES - 2 - spot, spot] = 1.0
    return table


def dot(left, right):
    return jnp.dot(left, right, preferred_element_type=F32)


def lane_ids(shape):
    return lax.broadcasted_iota(jnp.int32, shape, len(shape) - 1)


def pack_edges(value, row, low_ref, high_ref):
    place = (row + 16) % 64
    group = place // 32
    start = 4 * (place % 32)
    lane = lane_ids(value.shape)
    hit = (lane >= start) & (lane < start + 3)
    low = pltpu.roll(value, start, 1)
    high = pltpu.roll(value, lax.rem(start + 3, LANES), 1)
    low_ref[group] = jnp.where(hit, low, low_ref[group])
    high_ref[group] = jnp.where(hit, high, high_ref[group])


def send_edges(flags_ref, state_ref, low_ref, high_ref, row_refs, column_refs):
    height = state_ref.shape[0]
    even_row = flags_ref[0] == 0
    even_column = flags_ref[1] == 0
    row_refs[0][...] = state_ref[pl.ds(jnp.where(even_row, height - 3, 0), 3)]
    row_refs[1][...] = state_ref[pl.ds(jnp.where(even_row, 0, height - 3), 3)]
    column_refs[0][...] = jnp.where(even_column, high_ref[...], low_ref[...])
    column_refs[1][...] = jnp.where(even_column, low_ref[...], high_ref[...])


def prepare_kernel(blocks, coef_ref, table_ref, stem_ref, *outs):
    outs[-1][...] = stem_ref[...]
    spot = lax.broadcasted_iota(jnp.int32, (coef_ref.shape[2], LANES), 0)
    phase = lane_ids((coef_ref.shape[2], LANES)) % 4
    for block in range(blocks):
        mix_ref, side_ref, gain_ref, bias_ref = outs[4 * block:4 * block + 4]
        coef = coef_ref[block]
        for tap in range(7):
            mix_ref[tap] = dot(coef, table_ref[:, tap * 256:(tap + 1) * 256]).astype(BF16)
        for pair in range(21):
            tables = []
            for entry in (2 * pair, 2 * pair + 1):
                side, row, tap = entry // 21, entry % 21 // 3, entry % 3
                source = row * 7 + (tap if side == 0 else 6 - tap)
                inside = phase <= 2 - tap if side == 0 else (phase >= tap) & (phase <= 2)
                tables.append(jnp.where(((spot == source) | (spot == source + 49)) & inside, 1.0, 0.0).astype(BF16))
            out = dot(coef, jnp.concatenate(tables, axis=1)).astype(BF16)
            side_ref[2 * pair] = out[:, :LANES]
            side_ref[2 * pair + 1] = out[:, LANES:]
        out = dot(coef, table_ref[:, 1792:2176])
        gain_ref[...] = out[:, :LANES]
        bias_ref[0] = out[:, LANES:2 * LANES]
        bias_ref[1] = out[:, 2 * LANES:]


def prepare_table():
    table = np.zeros((160, 2176))
    angle = 2.0 * np.pi * np.arange(HALF + 1)[None, :] * (np.arange(7)[:, None] - 3) / LANES
    cos, sin = np.cos(angle), np.sin(angle)
    none = np.zeros((7, 1))
    real = np.concatenate([cos, cos[:, 1:HALF]], axis=1)
    imag = np.concatenate([none, -sin[:, 1:HALF], none, sin[:, 1:HALF]], axis=1)
    wave = np.concatenate([real, imag], axis=1)
    wave_high = wave.astype(BF16).astype(np.float64)
    for row in range(7):
        for tap in range(7):
            spot = row * 7 + tap
            table[spot, row * 256:(row + 1) * 256] = wave_high[tap]
            table[49 + spot, row * 256:(row + 1) * 256] = wave_high[tap]
            table[98 + spot, row * 256:(row + 1) * 256] = wave[tap] - wave_high[tap]
    table[147:150, 1792:1920] = 1.0
    table[150, 1920:2048] = 1.0
    table[151, 2048:2176] = 1.0
    return table


def stem_kernel(rows_ref, flags_ref, owner_ref, arrived_ref, weight_ref, state_ref, row_even_ref, row_odd_ref,
                column_even_ref, column_odd_ref, inverse_ref, split_ref, low_ref, high_ref):
    pieces = arrived_ref.shape[0]
    flux = arrived_ref.shape[1]
    step = 32

    def invert(index, _):
        for at in range(8):
            inverse_ref[owner_ref[index * 8 + at]] = index * 8 + at
        return 0

    lax.fori_loop(0, pieces // 8, invert, 0)
    source = lax.broadcasted_iota(jnp.int32, (2 * LANES, 2 * LANES), 0)
    target = lane_ids((2 * LANES, 2 * LANES))
    wanted = jnp.where(target < LANES, 2 * target, 2 * target - (2 * LANES - 1))
    table = jnp.where(source == wanted, 1.0, 0.0).astype(BF16)

    def split(index, _):
        part = arrived_ref[pl.ds(index * step, step)].reshape(step * flux, 2 * LANES)
        split_ref[pl.ds(index * step, step)] = dot(part, table).astype(BF16).reshape(step, flux, 2 * LANES)
        return 0

    lax.fori_loop(0, pieces // step, split, 0)
    state_ref[...] = jnp.zeros_like(state_ref)
    low_ref[...] = jnp.zeros_like(low_ref)
    high_ref[...] = jnp.zeros_like(high_ref)

    def group(index, _):
        rows = [rows_ref[1 + GROUP * index + at] for at in range(GROUP)]
        columns = []
        for row in rows:
            one = split_ref[inverse_ref[2 * row]]
            two = split_ref[inverse_ref[2 * row + 1]]
            columns.append(jnp.concatenate([one[:, :LANES], one[:, LANES:], two[:, :LANES], two[:, LANES:]], axis=0))
        out = dot(weight_ref[...], jnp.concatenate(columns, axis=1))
        for at, row in enumerate(rows):
            value = out[:, at * LANES:(at + 1) * LANES].astype(BF16)
            state_ref[row] = value
            pack_edges(value, row, low_ref, high_ref)
        return 0

    @pl.when(rows_ref[0] > 0)
    def _():
        lax.fori_loop(0, MOST // GROUP, group, 0)

    send_edges(flags_ref, state_ref, low_ref, high_ref, (row_even_ref, row_odd_ref), (column_even_ref, column_odd_ref))


def transform_kernel(state_ref, forward_ref, wave_ref):
    rows, width, _ = state_ref.shape
    part = state_ref[...].reshape(rows * width, LANES)
    wave_ref[...] = dot(part, forward_ref[...]).astype(BF16).reshape(rows, width, 2 * LANES)


def tree_sum(terms):
    while len(terms) > 1:
        terms = [a + b for a, b in zip(terms[::2], terms[1::2])] + terms[len(terms) - len(terms) % 2:]
    return terms[0]


def product_kernel(first, rows_ref, wave_ref, mix_ref, after_ref, prod_ref, *rest):
    height, width, _ = wave_ref.shape
    if rest:
        rest[0][0:6] = wave_ref[0:6]
        rest[0][6:12] = wave_ref[height - 6:height]

    def channel_band(band, _):
        span = pl.ds(pl.multiple_of((band + first) * 16, 16), 16)
        target = pl.ds(pl.multiple_of(band * 16, 16), 16)
        weights = [mix_ref[tap, span] for tap in range(7)]

        def some_rows(index, _):
            for at in range(UNROLL):
                spot = index * UNROLL + at
                base = jnp.clip(rows_ref[1 + spot] - 3, 0, height - 7)
                terms = []
                for tap in range(7):
                    wave = wave_ref[base + tap, span]
                    terms.append(wave[:, :LANES] * weights[tap][:, :LANES])
                    terms.append(wave[:, LANES:] * weights[tap][:, LANES:])
                prod_ref[spot, target] = tree_sum(terms)
            return 0

        lax.fori_loop(0, MOST // UNROLL, some_rows, 0)
        return 0

    lax.fori_loop(0, prod_ref.shape[1] // 16, channel_band, 0)


def block_kernel(last, block, rows_ref, flags_ref, state_ref, prod_one_ref, prod_two_ref, edge_wave_ref, row_even_ref, row_odd_ref,
                 column_even_ref, column_odd_ref, own_even_ref, own_odd_ref, mix_ref, side_ref, gain_ref,
                 bias_ref, forward_ref, flipped_ref, inverse_ref, turn_ref, expand_ref, reduce_ref, *rest):
    if last:
        out_ref, halo_ref, fix_ref, edge_ref, grid_ref, normed_ref, held_ref, wet_ref, ready_ref, copy_sem = rest
    else:
        (out_ref, send_row_even_ref, send_row_odd_ref, send_column_even_ref, send_column_odd_ref,
         halo_ref, fix_ref, edge_ref, grid_ref, normed_ref, low_ref, high_ref) = rest
    height, width, _ = state_ref.shape
    channels = 200
    pitch = height + 8
    count = rows_ref[0]
    even_row = flags_ref[0] == 0
    even_column = flags_ref[1] == 0
    fold = flags_ref[2] != 0

    def wave_of(rows, table):
        return dot(rows.reshape(3 * width, LANES), table).astype(BF16).reshape(3, width, 2 * LANES)

    left = jnp.where(even_column, column_odd_ref[...], column_even_ref[...])
    right = jnp.where(even_column, column_even_ref[...], column_odd_ref[...])
    low = jnp.where(even_column, own_odd_ref[...], own_even_ref[...])
    high = jnp.where(even_column, own_even_ref[...], own_odd_ref[...])
    grid_ref[0, 0:2] = left - high
    grid_ref[1, 0:2] = right - low
    halo_ref[0:3] = wave_of(jnp.where(even_row, row_odd_ref[0:3], row_even_ref[0:3]), forward_ref[...])
    for side in range(2):
        grid_ref[side, 2] = jnp.where(even_row, row_odd_ref[3 + side], row_even_ref[3 + side])

    @pl.when(jnp.logical_not(fold))
    def _():
        halo_ref[3:6] = wave_of(jnp.where(even_row, row_even_ref[0:3], row_odd_ref[0:3]), forward_ref[...])
        for side in range(2):
            grid_ref[side, 3] = jnp.where(even_row, row_even_ref[3 + side], row_odd_ref[3 + side])

    @pl.when(fold)
    def _():
        waves = wave_of(row_odd_ref[0:3], flipped_ref[...])
        for m in range(3):
            halo_ref[3 + m] = waves[2 - m]
        for side in range(2):
            grid_ref[side, 3] = dot(row_odd_ref[4 - side], turn_ref[...]).astype(BF16)

    def corrections(index, _):
        span = pl.ds(pl.multiple_of(index * 16, 16), 16)
        lane = lane_ids((16, LANES))
        for side in range(2):
            totals = [jnp.where(lane % 4 == 3, bias_ref[side, span], 0.0)] * 2
            here, other = grid_ref[side, 0, span], grid_ref[side, 1, span]
            upward = jnp.where(lane < HALF, here, grid_ref[side, 3, span])
            downward = jnp.where(lane < HALF, grid_ref[side, 2, span], here)
            slabs = [here, other, upward, downward]
            turned = [[pltpu.roll(slab, (-tap if side == 0 else tap) % LANES, 1) if tap else slab for tap in range(3)]
                      for slab in slabs]
            for tap_row in range(7):
                shift = 4 * (tap_row - 3)
                weights = [side_ref[(side * 7 + tap_row) * 3 + tap, span] for tap in range(3)]

                def moved(at):
                    value = weights[0] * turned[at][0] + weights[1] * turned[at][1] + weights[2] * turned[at][2]
                    return pltpu.roll(value, -shift % LANES, 1) if shift else value

                first, second = moved(0), moved(1)
                if shift > 0:
                    inner = lane < LANES - shift
                    first, second = jnp.where(inner, first, second), jnp.where(inner, second, first)
                    first = jnp.where((lane < HALF) & (lane >= HALF - shift), moved(2), first)
                elif shift < 0:
                    inner = lane >= -shift
                    first, second = jnp.where(inner, first, second), jnp.where(inner, second, first)
                    first = jnp.where((lane >= HALF) & (lane < HALF - shift), moved(3), first)
                totals = [totals[0] + first.astype(F32), totals[1] + second.astype(F32)]
            for group in range(2):
                edge_ref[side, group, span] = totals[group].astype(BF16)
        return 0

    lax.fori_loop(0, width // 16, corrections, 0)

    def rim(band, _):
        span = pl.ds(pl.multiple_of(band * 16, 16), 16)
        weights = [mix_ref[tap, span] for tap in range(7)]
        for at in range(6):
            terms = []
            for tap in range(7):
                spot = (at if at < 3 else at - 3) + tap
                if at < 3:
                    wave = halo_ref[spot, span] if spot < 3 else edge_wave_ref[spot - 3, span]
                else:
                    wave = edge_wave_ref[6 + spot, span] if spot < 6 else halo_ref[spot - 3, span]
                terms.append(wave[:, :LANES] * weights[tap][:, :LANES])
                terms.append(wave[:, LANES:] * weights[tap][:, LANES:])
            fix_ref[at, span] = tree_sum(terms)
        return 0

    lax.fori_loop(0, width // 16, rim, 0)

    if last:
        wet_ref[...] = jnp.zeros_like(wet_ref)
    else:
        out_ref[...] = jnp.zeros_like(out_ref)
        low_ref[...] = jnp.zeros_like(low_ref)
        high_ref[...] = jnp.zeros_like(high_ref)

    def normalise(index, slot):
        lane = lane_ids((width, LANES))
        joined = []
        for at in range(GROUP):
            spot = GROUP * index + at
            row = rows_ref[1 + spot]
            place = (row + 16) % 64
            group = place // 32
            turn = lax.rem(LANES - 4 * (place % 32), LANES)
            left = pltpu.roll(edge_ref[0, group], turn, 1)
            right = pltpu.roll(edge_ref[1, group], lax.rem(turn + 4, LANES), 1)
            rim_row = (row < 3) | (row >= height - 3)
            fixed = fix_ref[jnp.clip(jnp.where(row < 3, row, row - (height - 6)), 0, 5)]
            prod = jnp.where(rim_row, fixed, jnp.concatenate([prod_one_ref[spot], prod_two_ref[spot]], axis=0))
            joined.append(jnp.concatenate([prod, jnp.where(lane < 4, left, right)], axis=1))
        depth = dot(jnp.concatenate(joined, axis=0), inverse_ref[...])
        for at in range(GROUP):
            real = depth[at * width:at * width + channels]
            center = jnp.mean(real, axis=0, keepdims=True)
            real = real - center
            spread = jnp.mean(real * real, axis=0, keepdims=True)
            normed = real * lax.rsqrt(spread + 1e-06) * gain_ref[0:channels]
            normed = jnp.concatenate([normed, jnp.ones((width - channels, LANES), F32)], axis=0).astype(BF16)
            normed_ref[slot, :, at * LANES:(at + 1) * LANES] = normed

    def pointwise(index, slot):
        half = dot(expand_ref[block], normed_ref[slot])
        half = half.astype(GELU)
        bend = jnp.tanh(half * (half * half * GELU(8.0 * 0.044715 * ROOT) + GELU(2.0 * ROOT)))
        hidden = (half + half * bend).astype(BF16)
        branch = dot(reduce_ref[block], hidden)
        for at in range(GROUP):
            row = rows_ref[1 + GROUP * index + at]
            value = branch[:, at * LANES:(at + 1) * LANES] + state_ref[row].astype(F32)[:channels]
            if last:
                held_ref[pl.ds(row, channels, stride=pitch), :] = value
                wet_ref[pl.ds(row, 1), :] = jnp.ones((1, LANES), F32)
            else:
                value = jnp.concatenate([value, jnp.zeros((width - channels, LANES), F32)], axis=0).astype(BF16)
                out_ref[row] = value
                pack_edges(value, row, low_ref, high_ref)

    @pl.when(count > 0)
    def _():
        groups = MOST // GROUP
        normalise(0, 0)
        for index in range(groups):
            if index < groups - 1:
                normalise(index + 1, (index + 1) % 2)
            pointwise(index, index % 2)

    if last:
        wet = wet_ref[...] > 0.0
        part = channels // PARTS
        copies = []
        for at in range(PARTS):
            def finish(index, _):
                base = at * part + index * 8
                value = held_ref[pl.ds(base * pitch, 8 * pitch), :].reshape(8, pitch, LANES)[:, :height]
                ready_ref[pl.ds(base, 8)] = jnp.where(wet[None], value, 0.0).astype(BF16)
                return 0

            lax.fori_loop(0, part // 8, finish, 0)
            span = pl.ds(at * part, part)
            copy = pltpu.make_async_copy(ready_ref.at[span], out_ref.at[span], copy_sem.at[at])
            copy.start()
            copies.append(copy)
        for copy in copies:
            copy.wait()
    else:
        send_edges(flags_ref, out_ref, low_ref, high_ref, (send_row_even_ref, send_row_odd_ref),
                   (send_column_even_ref, send_column_odd_ref))


GELU = jnp.bfloat16
MOST = 48
PARTS = 5
UNROLL = 24
EARLY = 4


def smem():
    return pl.BlockSpec(memory_space=pltpu.SMEM)


def vmem():
    return pl.BlockSpec(memory_space=pltpu.VMEM)


def shape(*dims, dtype=BF16):
    return jax.ShapeDtypeStruct(dims, dtype)


def params(mib):
    return pltpu.CompilerParams(vmem_limit_bytes=mib * 1024 * 1024)


def edge_shapes(width):
    return [shape(3, width, LANES), shape(3, width, LANES), shape(2, width, LANES), shape(2, width, LANES)]


def run_prepare(coef, table, stem):
    blocks, width, _ = coef.shape
    one = [shape(7, width, 256), shape(42, width, LANES), shape(width, LANES, dtype=F32), shape(2, width, LANES, dtype=F32)]
    return pl.pallas_call(
        functools.partial(prepare_kernel, blocks),
        out_shape=one * blocks + [shape(*stem.shape)],
        in_specs=[vmem()] * 3,
        out_specs=[vmem()] * (4 * blocks + 1),
        compiler_params=params(16),
        cost_estimate=pl.CostEstimate(flops=2 * blocks * width * 160 * 7552, bytes_accessed=10_000_000, transcendentals=0),
        name="prepare",
    )(coef, table, stem)


def run_stem(rows, flags, owner, arrived, weight, height, width):
    return pl.pallas_call(
        stem_kernel,
        out_shape=[shape(height, width, LANES)] + edge_shapes(width),
        in_specs=[smem(), smem(), smem(), vmem(), vmem()],
        out_specs=[vmem()] * 5,
        scratch_shapes=[
            pltpu.SMEM(owner.shape, jnp.int32),
            pltpu.VMEM(arrived.shape, BF16),
            pltpu.VMEM((2, width, LANES), BF16),
            pltpu.VMEM((2, width, LANES), BF16),
        ],
        compiler_params=params(24),
        name="stem",
    )(rows, flags, owner, arrived, weight)


def run_transform(state, forward):
    height, width, _ = state.shape
    return pl.pallas_call(
        transform_kernel,
        out_shape=shape(height, width, 2 * LANES),
        grid=(height // 16,),
        in_specs=[pl.BlockSpec((16, width, LANES), lambda i: (i, 0, 0)), pl.BlockSpec((LANES, 2 * LANES), lambda i: (0, 0))],
        out_specs=pl.BlockSpec((16, width, 2 * LANES), lambda i: (i, 0, 0)),
        compiler_params=params(24),
        cost_estimate=pl.CostEstimate(flops=2 * height * width * LANES * 256, bytes_accessed=10_000_000, transcendentals=0),
        name="transform",
    )(state, forward)


def run_product(rows, wave, mix, after, first, bands):
    _, width, _ = wave.shape
    edges = [shape(12, width, 2 * LANES)] if first else []
    return pl.pallas_call(
        functools.partial(product_kernel, first),
        out_shape=[shape(MOST, bands * 16, LANES)] + edges,
        in_specs=[smem(), vmem(), vmem(), pl.BlockSpec(memory_space=pl.ANY)],
        out_specs=[vmem()] * (1 + len(edges)),
        compiler_params=params(24),
        cost_estimate=pl.CostEstimate(flops=28 * MOST * bands * 16 * LANES, bytes_accessed=20_000_000, transcendentals=0),
        name="product",
    )(rows, wave, mix, after)


def corner_kernel(flags_ref, column_even_ref, column_odd_ref, own_even_ref, own_odd_ref, strip_even_ref, strip_odd_ref,
                  after_ref, row_even_ref, row_odd_ref):
    even_column = flags_ref[1] == 0
    one = column_even_ref[0] - own_odd_ref[0]
    two = column_odd_ref[0] - own_even_ref[0]
    for strip_ref, row_ref in ((strip_even_ref, row_even_ref), (strip_odd_ref, row_odd_ref)):
        row_ref[0:3] = strip_ref[...]
        row_ref[3] = jnp.where(even_column, two, one)
        row_ref[4] = jnp.where(even_column, one, two)


def run_corner(flags, column_even, column_odd, own_even, own_odd, strip_even, strip_odd, after):
    _, width, _ = own_even.shape
    return pl.pallas_call(
        corner_kernel,
        out_shape=[shape(5, width, LANES)] * 2,
        in_specs=[smem()] + [vmem()] * 6 + [pl.BlockSpec(memory_space=pl.ANY)],
        out_specs=[vmem()] * 2,
        compiler_params=params(16),
        cost_estimate=pl.CostEstimate(flops=1000, bytes_accessed=500_000, transcendentals=0),
        name="corner",
    )(flags, column_even, column_odd, own_even, own_odd, strip_even, strip_odd, after)


def run_block(last, block, rows, flags, state, *arrays):
    height, width, _ = state.shape
    if last:
        out_shape = [shape(200, height, LANES)]
        extra = [
            pltpu.VMEM((200 * (height + 8), LANES), F32),
            pltpu.VMEM((height, LANES), F32),
            pltpu.VMEM((200, height, LANES), BF16),
            pltpu.SemaphoreType.DMA((PARTS,)),
        ]
    else:
        out_shape = [shape(height, width, LANES)] + edge_shapes(width)
        extra = [pltpu.VMEM((2, width, LANES), BF16)] * 2
    return pl.pallas_call(
        functools.partial(block_kernel, last, block),
        out_shape=out_shape,
        in_specs=[smem(), smem()] + [vmem()] * (1 + len(arrays)),
        out_specs=[pl.BlockSpec(memory_space=pl.ANY) if last else vmem()] * len(out_shape),
        scratch_shapes=[
            pltpu.VMEM((6, width, 2 * LANES), BF16),
            pltpu.VMEM((6, width, LANES), BF16),
            pltpu.VMEM((2, 2, width, LANES), BF16),
            pltpu.VMEM((2, 4, width, LANES), BF16),
            pltpu.VMEM((2, width, GROUP * LANES), BF16),
        ] + extra,
        compiler_params=params(28),
        name="block",
    )(rows, flags, state, *arrays)


def wet_rows(wet):
    height = wet.shape[0]
    count = jnp.sum(wet)
    before = jnp.arange(height)[None, :] <= jnp.arange(height)[:, None]
    rank = jnp.sum(jnp.where(before, wet[None, :], 0), axis=1) - 1
    spot = jnp.minimum(jnp.arange(MOST), count - 1)
    hits = (rank[None, :] == spot[:, None]) & (wet[None, :] > 0)
    rows = jnp.sum(jnp.where(hits, jnp.arange(height)[None, :], 0), axis=1)
    return jnp.concatenate([count[None], rows]).astype(jnp.int32)


def split_high(value):
    high = value.astype(BF16)
    return high, value - high.astype(F32)


def coefficients(depth_weight, depth_bias, norm_gain, width):
    blocks, channels = depth_bias.shape
    taps, rest = split_high(depth_weight.reshape(blocks, channels, 49))
    gain_one, left = split_high(norm_gain[:, :, None])
    gain_two, left = split_high(left)
    bias_one, bias_left = split_high(depth_bias[:, :, None])
    parts = [taps, rest.astype(BF16), taps, gain_one, gain_two, left.astype(BF16), bias_one, bias_left.astype(BF16)]
    coef = jnp.concatenate(parts, axis=2)
    return jnp.pad(coef, ((0, 0), (0, width - channels), (0, 160 - coef.shape[2])))


def pointwise_weights(expand_weight, expand_bias, reduce_weight, width):
    blocks, channels, hidden = expand_weight.shape
    spare = width - channels
    high, low = split_high(0.5 * expand_bias[:, None, :])
    expand = jnp.concatenate(
        [expand_weight * BF16(0.5), high, low.astype(BF16), jnp.zeros((blocks, spare - 2, hidden), BF16)], axis=1
    )
    return jnp.transpose(lax.optimization_barrier(expand), (0, 2, 1)), jnp.transpose(reduce_weight, (0, 2, 1))


def body(
    atm_flux,
    owner_map,
    wet_mask,
    stem_weight,
    depth_weight,
    depth_bias,
    norm_gain,
    expand_weight,
    expand_bias,
    reduce_weight,
):
    lon_count = lax.axis_size("gx")
    lat_count = lax.axis_size("gy")
    lon_index = lax.axis_index("gx")
    lat_index = lax.axis_index("gy")
    blocks, channels = depth_bias.shape
    width = (channels + 15) // 16 * 16
    height = wet_mask.shape[0]
    arrived = lax.all_to_all(atm_flux[0], ("gx", "gy"), split_axis=0, concat_axis=0, tiled=True)[:, 0]
    owner = owner_map[:, 0]
    rows = wet_rows(wet_mask[:, 0])
    flags = jnp.stack([lat_index % 2, lon_index % 2, lat_index == lat_count - 1]).astype(jnp.int32)
    stem = jnp.transpose(stem_weight, (0, 2, 3, 1)).reshape(channels, -1)
    stem = jnp.pad(stem, ((0, width - channels), (0, 0)))
    forward, back = fourier_tables()
    flipped = jnp.asarray(forward[::-1], BF16)
    forward = jnp.asarray(forward, BF16)
    back = jnp.asarray(back, BF16)
    turn = jnp.asarray(fold_table(), BF16)
    coef = coefficients(depth_weight, depth_bias, norm_gain, width)
    prepared = run_prepare(coef, jnp.asarray(prepare_table(), BF16), stem)
    expand, reduce = pointwise_weights(expand_weight, expand_bias, reduce_weight, width)
    arrived, expand = lax.optimization_barrier((arrived, expand))
    state, *edges = run_stem(rows, flags, owner, arrived, prepared[-1], height, width)
    lon_even = [(i, i ^ 1) for i in range(lon_count)]
    lon_odd = [(i, ((i - 1 ^ 1) + 1) % lon_count) for i in range(lon_count)]
    lat_even = [(i, i ^ 1) for i in range(lat_count)]
    top = lat_count - 1
    lat_odd = []
    for lon in range(lon_count):
        for lat in range(1, top):
            lat_odd.append((lon * lat_count + lat, lon * lat_count + (lat - 1 ^ 1) + 1))
        lat_odd.append((lon * lat_count + top, (lon_count - 1 - lon) * lat_count + top))
    for index in range(blocks):
        last = index == blocks - 1
        row_even, row_odd, own_even, own_odd = edges
        column_even = lax.ppermute(own_even, "gx", lon_even)
        column_odd = lax.ppermute(own_odd, "gx", lon_odd)
        mix, side, gain, bias = prepared[4 * index:4 * index + 4]
        bands = width // 16
        wave = run_transform(state, forward)
        prod = run_product(rows, wave, mix, wave, 0, EARLY)
        row_even, row_odd = run_corner(flags, column_even, column_odd, own_even, own_odd, row_even, row_odd, prod[0])
        prod += run_product(rows, wave, mix, row_odd, EARLY, bands - EARLY)
        row_even = lax.ppermute(row_even, "gy", lat_even)
        row_odd = lax.ppermute(row_odd, ("gx", "gy"), lat_odd)
        out = run_block(
            last, index, rows, flags, state, *prod, row_even, row_odd, column_even, column_odd,
            own_even, own_odd, mix, side, gain, bias, forward, flipped, back, turn,
            expand, reduce,
        )
        if last:
            return out[0]
        state, *edges = out


def solution(mesh):
    return jax.shard_map(
        body,
        mesh=mesh,
        in_specs=(
            P(("gx", "gy"), None, None, None, None),
            P(None, ("gx", "gy")),
            P("gy", "gx"),
            P(),
            P(),
            P(),
            P(),
            P(),
            P(),
            P(),
        ),
        out_specs=P(None, "gy", "gx"),
        check_vma=False,
    )
```

```python
import functools

import jax
import jax.numpy as jnp
import numpy as np
from jax import lax
from jax.experimental import pallas as pl
from jax.experimental.pallas import tpu as pltpu
from jax.sharding import PartitionSpec as P

LANES = 128
GROUP = 8
HALF = LANES // 2
ROOT = float(np.sqrt(2.0 / np.pi))
BF16 = jnp.bfloat16
F32 = jnp.float32


def fourier_tables():
    spot = np.arange(LANES)[:, None]
    wave = np.arange(HALF)[None, :]
    angle = 2.0 * np.pi * (spot * wave % LANES) / LANES
    cos, sin = np.cos(angle), np.sin(angle)
    plain = np.concatenate([cos, -sin], axis=1)
    plain[:, HALF] = np.where(np.arange(LANES) % 2 == 0, 1.0, -1.0)
    swapped = np.concatenate([-sin, cos], axis=1)
    swapped[:, 0] = 0.0
    swapped[:, HALF] = 0.0
    forward = np.concatenate([plain, swapped], axis=1)
    inverse = plain.T * (2.0 / LANES)
    inverse[0] /= 2.0
    inverse[HALF] /= 2.0
    edges = np.zeros((LANES, LANES))
    for j in range(3):
        edges[j, j] = 1.0
        edges[4 + j, LANES - 3 + j] = 1.0
    edges[3, :] = 1.0
    edges[7, :] = 1.0
    inverse = np.concatenate([inverse, edges], axis=0)
    return forward, inverse


def fold_table():
    table = np.zeros((LANES, LANES))
    spot = np.arange(LANES - 1)
    table[LANES - 2 - spot, spot] = 1.0
    return table


def dot(left, right):
    return jnp.dot(left, right, preferred_element_type=F32)


def lane_ids(shape):
    return lax.broadcasted_iota(jnp.int32, shape, len(shape) - 1)


def pack_edges(value, row, low_ref, high_ref):
    place = (row + 16) % 64
    group = place // 32
    start = 4 * (place % 32)
    lane = lane_ids(value.shape)
    hit = (lane >= start) & (lane < start + 3)
    low = pltpu.roll(value, start, 1)
    high = pltpu.roll(value, lax.rem(start + 3, LANES), 1)
    low_ref[group] = jnp.where(hit, low, low_ref[group])
    high_ref[group] = jnp.where(hit, high, high_ref[group])


def send_edges(flags_ref, state_ref, low_ref, high_ref, row_refs, column_refs):
    height = state_ref.shape[0]
    even_row = flags_ref[0] == 0
    even_column = flags_ref[1] == 0
    row_refs[0][...] = state_ref[pl.ds(jnp.where(even_row, height - 3, 0), 3)]
    row_refs[1][...] = state_ref[pl.ds(jnp.where(even_row, 0, height - 3), 3)]
    column_refs[0][...] = jnp.where(even_column, high_ref[...], low_ref[...])
    column_refs[1][...] = jnp.where(even_column, low_ref[...], high_ref[...])


def prepare_kernel(blocks, coef_ref, table_ref, stem_ref, *outs):
    outs[-1][...] = stem_ref[...]
    spot = lax.broadcasted_iota(jnp.int32, (coef_ref.shape[2], LANES), 0)
    phase = lane_ids((coef_ref.shape[2], LANES)) % 4
    for block in range(blocks):
        mix_ref, side_ref, gain_ref, bias_ref = outs[4 * block:4 * block + 4]
        coef = coef_ref[block]
        for tap in range(7):
            mix_ref[tap] = dot(coef, table_ref[:, tap * 256:(tap + 1) * 256]).astype(BF16)
        for pair in range(21):
            tables = []
            for entry in (2 * pair, 2 * pair + 1):
                side, row, tap = entry // 21, entry % 21 // 3, entry % 3
                source = row * 7 + (tap if side == 0 else 6 - tap)
                inside = phase <= 2 - tap if side == 0 else (phase >= tap) & (phase <= 2)
                tables.append(jnp.where(((spot == source) | (spot == source + 49)) & inside, 1.0, 0.0).astype(BF16))
            out = dot(coef, jnp.concatenate(tables, axis=1)).astype(BF16)
            side_ref[2 * pair] = out[:, :LANES]
            side_ref[2 * pair + 1] = out[:, LANES:]
        out = dot(coef, table_ref[:, 1792:2176])
        gain_ref[...] = out[:, :LANES]
        bias_ref[0] = out[:, LANES:2 * LANES]
        bias_ref[1] = out[:, 2 * LANES:]


def prepare_table():
    table = np.zeros((160, 2176))
    angle = 2.0 * np.pi * np.arange(HALF + 1)[None, :] * (np.arange(7)[:, None] - 3) / LANES
    cos, sin = np.cos(angle), np.sin(angle)
    none = np.zeros((7, 1))
    real = np.concatenate([cos, cos[:, 1:HALF]], axis=1)
    imag = np.concatenate([none, -sin[:, 1:HALF], none, sin[:, 1:HALF]], axis=1)
    wave = np.concatenate([real, imag], axis=1)
    wave_high = wave.astype(BF16).astype(np.float64)
    for row in range(7):
        for tap in range(7):
            spot = row * 7 + tap
            table[spot, row * 256:(row + 1) * 256] = wave_high[tap]
            table[49 + spot, row * 256:(row + 1) * 256] = wave_high[tap]
            table[98 + spot, row * 256:(row + 1) * 256] = wave[tap] - wave_high[tap]
    table[147:150, 1792:1920] = 1.0
    table[150, 1920:2048] = 1.0
    table[151, 2048:2176] = 1.0
    return table


def stem_kernel(rows_ref, flags_ref, owner_ref, arrived_ref, weight_ref, state_ref, row_even_ref, row_odd_ref,
                column_even_ref, column_odd_ref, inverse_ref, split_ref, low_ref, high_ref, held_weight_ref, weight_sem):
    copy = pltpu.make_async_copy(weight_ref, held_weight_ref, weight_sem)
    copy.start()
    pieces = arrived_ref.shape[0]
    flux = arrived_ref.shape[1]
    step = 32

    def invert(index, _):
        for at in range(8):
            inverse_ref[owner_ref[index * 8 + at]] = index * 8 + at
        return 0

    lax.fori_loop(0, pieces // 8, invert, 0)
    source = lax.broadcasted_iota(jnp.int32, (2 * LANES, 2 * LANES), 0)
    target = lane_ids((2 * LANES, 2 * LANES))
    wanted = jnp.where(target < LANES, 2 * target, 2 * target - (2 * LANES - 1))
    table = jnp.where(source == wanted, 1.0, 0.0).astype(BF16)

    def split(index, _):
        part = arrived_ref[pl.ds(index * step, step)].reshape(step * flux, 2 * LANES)
        split_ref[pl.ds(index * step, step)] = dot(part, table).astype(BF16).reshape(step, flux, 2 * LANES)
        return 0

    lax.fori_loop(0, pieces // step, split, 0)
    copy.wait()
    state_ref[...] = jnp.zeros_like(state_ref)
    low_ref[...] = jnp.zeros_like(low_ref)
    high_ref[...] = jnp.zeros_like(high_ref)

    def group(index, _):
        rows = [rows_ref[1 + GROUP * index + at] for at in range(GROUP)]
        columns = []
        for row in rows:
            one = split_ref[inverse_ref[2 * row]]
            two = split_ref[inverse_ref[2 * row + 1]]
            columns.append(jnp.concatenate([one[:, :LANES], one[:, LANES:], two[:, :LANES], two[:, LANES:]], axis=0))
        out = dot(held_weight_ref[...], jnp.concatenate(columns, axis=1))
        for at, row in enumerate(rows):
            value = out[:, at * LANES:(at + 1) * LANES].astype(BF16)
            state_ref[row] = value
            pack_edges(value, row, low_ref, high_ref)
        return 0

    @pl.when(rows_ref[0] > 0)
    def _():
        lax.fori_loop(0, MOST // GROUP, group, 0)

    send_edges(flags_ref, state_ref, low_ref, high_ref, (row_even_ref, row_odd_ref), (column_even_ref, column_odd_ref))


def transform_kernel(state_ref, forward_ref, wave_ref):
    rows, width, _ = state_ref.shape
    part = state_ref[...].reshape(rows * width, LANES)
    wave_ref[...] = dot(part, forward_ref[...]).astype(BF16).reshape(rows, width, 2 * LANES)


def tree_sum(terms):
    while len(terms) > 1:
        terms = [a + b for a, b in zip(terms[::2], terms[1::2])] + terms[len(terms) - len(terms) % 2:]
    return terms[0]


def product_kernel(first, rows_ref, wave_ref, mix_ref, after_ref, prod_ref, *rest):
    height, width, _ = wave_ref.shape
    if rest:
        rest[0][0:6] = wave_ref[0:6]
        rest[0][6:12] = wave_ref[height - 6:height]

    def channel_band(band, _):
        span = pl.ds(pl.multiple_of((band + first) * 16, 16), 16)
        target = pl.ds(pl.multiple_of(band * 16, 16), 16)
        weights = [mix_ref[tap, span] for tap in range(7)]

        def some_rows(index, _):
            for at in range(UNROLL):
                spot = index * UNROLL + at
                base = jnp.clip(rows_ref[1 + spot] - 3, 0, height - 7)
                terms = []
                for tap in range(7):
                    wave = wave_ref[base + tap, span]
                    terms.append(wave[:, :LANES] * weights[tap][:, :LANES])
                    terms.append(wave[:, LANES:] * weights[tap][:, LANES:])
                prod_ref[spot, target] = tree_sum(terms)
            return 0

        lax.fori_loop(0, MOST // UNROLL, some_rows, 0)
        return 0

    lax.fori_loop(0, prod_ref.shape[1] // 16, channel_band, 0)


def block_kernel(last, block, rows_ref, flags_ref, state_ref, prod_one_ref, prod_two_ref, edge_wave_ref, row_even_ref, row_odd_ref,
                 column_even_ref, column_odd_ref, own_even_ref, own_odd_ref, mix_ref, side_ref, gain_ref,
                 bias_ref, forward_ref, flipped_ref, inverse_ref, turn_ref, expand_ref, reduce_ref, *rest):
    if last:
        out_ref, halo_ref, fix_ref, edge_ref, grid_ref, normed_ref, held_ref, wet_ref, ready_ref, copy_sem = rest
    else:
        (out_ref, send_row_even_ref, send_row_odd_ref, send_column_even_ref, send_column_odd_ref,
         halo_ref, fix_ref, edge_ref, grid_ref, normed_ref, low_ref, high_ref) = rest
    height, width, _ = state_ref.shape
    channels = 200
    pitch = height + 8
    count = rows_ref[0]
    even_row = flags_ref[0] == 0
    even_column = flags_ref[1] == 0
    fold = flags_ref[2] != 0

    def wave_of(rows, table):
        return dot(rows.reshape(3 * width, LANES), table).astype(BF16).reshape(3, width, 2 * LANES)

    left = jnp.where(even_column, column_odd_ref[...], column_even_ref[...])
    right = jnp.where(even_column, column_even_ref[...], column_odd_ref[...])
    low = jnp.where(even_column, own_odd_ref[...], own_even_ref[...])
    high = jnp.where(even_column, own_even_ref[...], own_odd_ref[...])
    grid_ref[0, 0:2] = left - high
    grid_ref[1, 0:2] = right - low
    halo_ref[0:3] = wave_of(jnp.where(even_row, row_odd_ref[0:3], row_even_ref[0:3]), forward_ref[...])
    for side in range(2):
        grid_ref[side, 2] = jnp.where(even_row, row_odd_ref[3 + side], row_even_ref[3 + side])

    @pl.when(jnp.logical_not(fold))
    def _():
        halo_ref[3:6] = wave_of(jnp.where(even_row, row_even_ref[0:3], row_odd_ref[0:3]), forward_ref[...])
        for side in range(2):
            grid_ref[side, 3] = jnp.where(even_row, row_even_ref[3 + side], row_odd_ref[3 + side])

    @pl.when(fold)
    def _():
        waves = wave_of(row_odd_ref[0:3], flipped_ref[...])
        for m in range(3):
            halo_ref[3 + m] = waves[2 - m]
        for side in range(2):
            grid_ref[side, 3] = dot(row_odd_ref[4 - side], turn_ref[...]).astype(BF16)

    def corrections(index, _):
        span = pl.ds(pl.multiple_of(index * 16, 16), 16)
        lane = lane_ids((16, LANES))
        for side in range(2):
            totals = [jnp.where(lane % 4 == 3, bias_ref[side, span], 0.0)] * 2
            here, other = grid_ref[side, 0, span], grid_ref[side, 1, span]
            upward = jnp.where(lane < HALF, here, grid_ref[side, 3, span])
            downward = jnp.where(lane < HALF, grid_ref[side, 2, span], here)
            slabs = [here, other, upward, downward]
            turned = [[pltpu.roll(slab, (-tap if side == 0 else tap) % LANES, 1) if tap else slab for tap in range(3)]
                      for slab in slabs]
            for tap_row in range(7):
                shift = 4 * (tap_row - 3)
                weights = [side_ref[(side * 7 + tap_row) * 3 + tap, span] for tap in range(3)]

                def moved(at):
                    value = weights[0] * turned[at][0] + weights[1] * turned[at][1] + weights[2] * turned[at][2]
                    return pltpu.roll(value, -shift % LANES, 1) if shift else value

                first, second = moved(0), moved(1)
                if shift > 0:
                    inner = lane < LANES - shift
                    first, second = jnp.where(inner, first, second), jnp.where(inner, second, first)
                    first = jnp.where((lane < HALF) & (lane >= HALF - shift), moved(2), first)
                elif shift < 0:
                    inner = lane >= -shift
                    first, second = jnp.where(inner, first, second), jnp.where(inner, second, first)
                    first = jnp.where((lane >= HALF) & (lane < HALF - shift), moved(3), first)
                totals = [totals[0] + first.astype(F32), totals[1] + second.astype(F32)]
            for group in range(2):
                edge_ref[side, group, span] = totals[group].astype(BF16)
        return 0

    lax.fori_loop(0, width // 16, corrections, 0)

    def rim(band, _):
        span = pl.ds(pl.multiple_of(band * 16, 16), 16)
        weights = [mix_ref[tap, span] for tap in range(7)]
        for at in range(6):
            terms = []
            for tap in range(7):
                spot = (at if at < 3 else at - 3) + tap
                if at < 3:
                    wave = halo_ref[spot, span] if spot < 3 else edge_wave_ref[spot - 3, span]
                else:
                    wave = edge_wave_ref[6 + spot, span] if spot < 6 else halo_ref[spot - 3, span]
                terms.append(wave[:, :LANES] * weights[tap][:, :LANES])
                terms.append(wave[:, LANES:] * weights[tap][:, LANES:])
            fix_ref[at, span] = tree_sum(terms)
        return 0

    lax.fori_loop(0, width // 16, rim, 0)

    if last:
        wet_ref[...] = jnp.zeros_like(wet_ref)
    else:
        out_ref[...] = jnp.zeros_like(out_ref)
        low_ref[...] = jnp.zeros_like(low_ref)
        high_ref[...] = jnp.zeros_like(high_ref)

    def normalise(index, slot):
        lane = lane_ids((width, LANES))
        joined = []
        for at in range(GROUP):
            spot = GROUP * index + at
            row = rows_ref[1 + spot]
            place = (row + 16) % 64
            group = place // 32
            turn = lax.rem(LANES - 4 * (place % 32), LANES)
            left = pltpu.roll(edge_ref[0, group], turn, 1)
            right = pltpu.roll(edge_ref[1, group], lax.rem(turn + 4, LANES), 1)
            rim_row = (row < 3) | (row >= height - 3)
            fixed = fix_ref[jnp.clip(jnp.where(row < 3, row, row - (height - 6)), 0, 5)]
            prod = jnp.where(rim_row, fixed, jnp.concatenate([prod_one_ref[spot], prod_two_ref[spot]], axis=0))
            joined.append(jnp.concatenate([prod, jnp.where(lane < 4, left, right)], axis=1))
        depth = dot(jnp.concatenate(joined, axis=0), inverse_ref[...])
        for at in range(GROUP):
            real = depth[at * width:at * width + channels]
            center = jnp.mean(real, axis=0, keepdims=True)
            real = real - center
            spread = jnp.mean(real * real, axis=0, keepdims=True)
            normed = real * lax.rsqrt(spread + 1e-06) * gain_ref[0:channels]
            normed = jnp.concatenate([normed, jnp.ones((width - channels, LANES), F32)], axis=0).astype(BF16)
            normed_ref[slot, :, at * LANES:(at + 1) * LANES] = normed

    def pointwise(index, slot):
        half = dot(expand_ref[block], normed_ref[slot])
        half = half.astype(GELU)
        bend = jnp.tanh(half * (half * half * GELU(8.0 * 0.044715 * ROOT) + GELU(2.0 * ROOT)))
        hidden = (half + half * bend).astype(BF16)
        branch = dot(reduce_ref[block], hidden)
        for at in range(GROUP):
            row = rows_ref[1 + GROUP * index + at]
            value = branch[:, at * LANES:(at + 1) * LANES] + state_ref[row].astype(F32)[:channels]
            if last:
                held_ref[pl.ds(row, channels, stride=pitch), :] = value
                wet_ref[pl.ds(row, 1), :] = jnp.ones((1, LANES), F32)
            else:
                value = jnp.concatenate([value, jnp.zeros((width - channels, LANES), F32)], axis=0).astype(BF16)
                out_ref[row] = value
                pack_edges(value, row, low_ref, high_ref)

    @pl.when(count > 0)
    def _():
        groups = MOST // GROUP
        normalise(0, 0)
        for index in range(groups):
            if index < groups - 1:
                normalise(index + 1, (index + 1) % 2)
            pointwise(index, index % 2)

    if last:
        wet = wet_ref[...] > 0.0
        part = channels // PARTS
        copies = []
        for at in range(PARTS):
            def finish(index, _):
                base = at * part + index * 8
                value = held_ref[pl.ds(base * pitch, 8 * pitch), :].reshape(8, pitch, LANES)[:, :height]
                ready_ref[pl.ds(base, 8)] = jnp.where(wet[None], value, 0.0).astype(BF16)
                return 0

            lax.fori_loop(0, part // 8, finish, 0)
            span = pl.ds(at * part, part)
            copy = pltpu.make_async_copy(ready_ref.at[span], out_ref.at[span], copy_sem.at[at])
            copy.start()
            copies.append(copy)
        for copy in copies:
            copy.wait()
    else:
        send_edges(flags_ref, out_ref, low_ref, high_ref, (send_row_even_ref, send_row_odd_ref),
                   (send_column_even_ref, send_column_odd_ref))


GELU = jnp.bfloat16
MOST = 48
PARTS = 5
UNROLL = 24
EARLY = 4


def smem():
    return pl.BlockSpec(memory_space=pltpu.SMEM)


def vmem():
    return pl.BlockSpec(memory_space=pltpu.VMEM)


def shape(*dims, dtype=BF16):
    return jax.ShapeDtypeStruct(dims, dtype)


def params(mib):
    return pltpu.CompilerParams(vmem_limit_bytes=mib * 1024 * 1024)


def edge_shapes(width):
    return [shape(3, width, LANES), shape(3, width, LANES), shape(2, width, LANES), shape(2, width, LANES)]


def run_prepare(coef, table, stem):
    blocks, width, _ = coef.shape
    one = [shape(7, width, 256), shape(42, width, LANES), shape(width, LANES, dtype=F32), shape(2, width, LANES, dtype=F32)]
    return pl.pallas_call(
        functools.partial(prepare_kernel, blocks),
        out_shape=one * blocks + [shape(*stem.shape)],
        in_specs=[vmem()] * 3,
        out_specs=[vmem()] * (4 * blocks + 1),
        compiler_params=params(16),
        cost_estimate=pl.CostEstimate(flops=2 * blocks * width * 160 * 7552, bytes_accessed=10_000_000, transcendentals=0),
        name="prepare",
    )(coef, table, stem)


def run_stem(rows, flags, owner, arrived, weight, height, width):
    return pl.pallas_call(
        stem_kernel,
        out_shape=[shape(height, width, LANES)] + edge_shapes(width),
        in_specs=[smem(), smem(), smem(), vmem(), pl.BlockSpec(memory_space=pl.ANY)],
        out_specs=[vmem()] * 5,
        scratch_shapes=[
            pltpu.SMEM(owner.shape, jnp.int32),
            pltpu.VMEM(arrived.shape, BF16),
            pltpu.VMEM((2, width, LANES), BF16),
            pltpu.VMEM((2, width, LANES), BF16),
            pltpu.VMEM(weight.shape, BF16),
            pltpu.SemaphoreType.DMA,
        ],
        compiler_params=params(24),
        name="stem",
    )(rows, flags, owner, arrived, weight)


def run_transform(state, forward):
    height, width, _ = state.shape
    return pl.pallas_call(
        transform_kernel,
        out_shape=shape(height, width, 2 * LANES),
        grid=(height // 16,),
        in_specs=[pl.BlockSpec((16, width, LANES), lambda i: (i, 0, 0)), pl.BlockSpec((LANES, 2 * LANES), lambda i: (0, 0))],
        out_specs=pl.BlockSpec((16, width, 2 * LANES), lambda i: (i, 0, 0)),
        compiler_params=params(24),
        cost_estimate=pl.CostEstimate(flops=2 * height * width * LANES * 256, bytes_accessed=10_000_000, transcendentals=0),
        name="transform",
    )(state, forward)


def run_product(rows, wave, mix, after, first, bands):
    _, width, _ = wave.shape
    edges = [shape(12, width, 2 * LANES)] if first else []
    return pl.pallas_call(
        functools.partial(product_kernel, first),
        out_shape=[shape(MOST, bands * 16, LANES)] + edges,
        in_specs=[smem(), vmem(), vmem(), pl.BlockSpec(memory_space=pl.ANY)],
        out_specs=[vmem()] * (1 + len(edges)),
        compiler_params=params(24),
        cost_estimate=pl.CostEstimate(flops=28 * MOST * bands * 16 * LANES, bytes_accessed=20_000_000, transcendentals=0),
        name="product",
    )(rows, wave, mix, after)


def corner_kernel(flags_ref, column_even_ref, column_odd_ref, own_even_ref, own_odd_ref, strip_even_ref, strip_odd_ref,
                  after_ref, row_even_ref, row_odd_ref):
    even_column = flags_ref[1] == 0
    one = column_even_ref[0] - own_odd_ref[0]
    two = column_odd_ref[0] - own_even_ref[0]
    for strip_ref, row_ref in ((strip_even_ref, row_even_ref), (strip_odd_ref, row_odd_ref)):
        row_ref[0:3] = strip_ref[...]
        row_ref[3] = jnp.where(even_column, two, one)
        row_ref[4] = jnp.where(even_column, one, two)


def run_corner(flags, column_even, column_odd, own_even, own_odd, strip_even, strip_odd, after):
    _, width, _ = own_even.shape
    return pl.pallas_call(
        corner_kernel,
        out_shape=[shape(5, width, LANES)] * 2,
        in_specs=[smem()] + [vmem()] * 6 + [pl.BlockSpec(memory_space=pl.ANY)],
        out_specs=[vmem()] * 2,
        compiler_params=params(16),
        cost_estimate=pl.CostEstimate(flops=1000, bytes_accessed=500_000, transcendentals=0),
        name="corner",
    )(flags, column_even, column_odd, own_even, own_odd, strip_even, strip_odd, after)


def run_block(last, block, rows, flags, state, *arrays):
    height, width, _ = state.shape
    if last:
        out_shape = [shape(200, height, LANES)]
        extra = [
            pltpu.VMEM((200 * (height + 8), LANES), F32),
            pltpu.VMEM((height, LANES), F32),
            pltpu.VMEM((200, height, LANES), BF16),
            pltpu.SemaphoreType.DMA((PARTS,)),
        ]
    else:
        out_shape = [shape(height, width, LANES)] + edge_shapes(width)
        extra = [pltpu.VMEM((2, width, LANES), BF16)] * 2
    return pl.pallas_call(
        functools.partial(block_kernel, last, block),
        out_shape=out_shape,
        in_specs=[smem(), smem()] + [vmem()] * (1 + len(arrays)),
        out_specs=[pl.BlockSpec(memory_space=pl.ANY) if last else vmem()] * len(out_shape),
        scratch_shapes=[
            pltpu.VMEM((6, width, 2 * LANES), BF16),
            pltpu.VMEM((6, width, LANES), BF16),
            pltpu.VMEM((2, 2, width, LANES), BF16),
            pltpu.VMEM((2, 4, width, LANES), BF16),
            pltpu.VMEM((2, width, GROUP * LANES), BF16),
        ] + extra,
        compiler_params=params(28),
        name="block",
    )(rows, flags, state, *arrays)


def wet_rows(wet):
    height = wet.shape[0]
    count = jnp.sum(wet)
    before = jnp.arange(height)[None, :] <= jnp.arange(height)[:, None]
    rank = jnp.sum(jnp.where(before, wet[None, :], 0), axis=1) - 1
    spot = jnp.minimum(jnp.arange(MOST), count - 1)
    hits = (rank[None, :] == spot[:, None]) & (wet[None, :] > 0)
    rows = jnp.sum(jnp.where(hits, jnp.arange(height)[None, :], 0), axis=1)
    return jnp.concatenate([count[None], rows]).astype(jnp.int32)


def split_high(value):
    high = value.astype(BF16)
    return high, value - high.astype(F32)


def coefficients(depth_weight, depth_bias, norm_gain, width):
    blocks, channels = depth_bias.shape
    taps, rest = split_high(depth_weight.reshape(blocks, channels, 49))
    gain_one, left = split_high(norm_gain[:, :, None])
    gain_two, left = split_high(left)
    bias_one, bias_left = split_high(depth_bias[:, :, None])
    parts = [taps, rest.astype(BF16), taps, gain_one, gain_two, left.astype(BF16), bias_one, bias_left.astype(BF16)]
    coef = jnp.concatenate(parts, axis=2)
    return jnp.pad(coef, ((0, 0), (0, width - channels), (0, 160 - coef.shape[2])))


def pointwise_weights(expand_weight, expand_bias, reduce_weight, width):
    blocks, channels, hidden = expand_weight.shape
    spare = width - channels
    high, low = split_high(0.5 * expand_bias[:, None, :])
    expand = jnp.concatenate(
        [expand_weight * BF16(0.5), high, low.astype(BF16), jnp.zeros((blocks, spare - 2, hidden), BF16)], axis=1
    )
    return jnp.transpose(lax.optimization_barrier(expand), (0, 2, 1)), jnp.transpose(reduce_weight, (0, 2, 1))


def body(
    atm_flux,
    owner_map,
    wet_mask,
    stem_weight,
    depth_weight,
    depth_bias,
    norm_gain,
    expand_weight,
    expand_bias,
    reduce_weight,
):
    lon_count = lax.axis_size("gx")
    lat_count = lax.axis_size("gy")
    lon_index = lax.axis_index("gx")
    lat_index = lax.axis_index("gy")
    blocks, channels = depth_bias.shape
    width = (channels + 15) // 16 * 16
    height = wet_mask.shape[0]
    arrived = lax.all_to_all(atm_flux[0], ("gx", "gy"), split_axis=0, concat_axis=0, tiled=True)[:, 0]
    owner = owner_map[:, 0]
    rows = wet_rows(wet_mask[:, 0])
    flags = jnp.stack([lat_index % 2, lon_index % 2, lat_index == lat_count - 1]).astype(jnp.int32)
    stem = jnp.transpose(stem_weight, (0, 2, 3, 1)).reshape(channels, -1)
    stem = jnp.pad(stem, ((0, width - channels), (0, 0)))
    forward, back = fourier_tables()
    flipped = jnp.asarray(forward[::-1], BF16)
    forward = jnp.asarray(forward, BF16)
    back = jnp.asarray(back, BF16)
    turn = jnp.asarray(fold_table(), BF16)
    coef = coefficients(depth_weight, depth_bias, norm_gain, width)
    prepared = run_prepare(coef, jnp.asarray(prepare_table(), BF16), stem)
    expand, reduce = pointwise_weights(expand_weight, expand_bias, reduce_weight, width)
    arrived, expand = lax.optimization_barrier((arrived, expand))
    state, *edges = run_stem(rows, flags, owner, arrived, prepared[-1], height, width)
    lon_even = [(i, i ^ 1) for i in range(lon_count)]
    lon_odd = [(i, ((i - 1 ^ 1) + 1) % lon_count) for i in range(lon_count)]
    lat_even = [(i, i ^ 1) for i in range(lat_count)]
    top = lat_count - 1
    lat_odd = []
    for lon in range(lon_count):
        for lat in range(1, top):
            lat_odd.append((lon * lat_count + lat, lon * lat_count + (lat - 1 ^ 1) + 1))
        lat_odd.append((lon * lat_count + top, (lon_count - 1 - lon) * lat_count + top))
    for index in range(blocks):
        last = index == blocks - 1
        row_even, row_odd, own_even, own_odd = edges
        column_even = lax.ppermute(own_even, "gx", lon_even)
        column_odd = lax.ppermute(own_odd, "gx", lon_odd)
        mix, side, gain, bias = prepared[4 * index:4 * index + 4]
        bands = width // 16
        wave = run_transform(state, forward)
        prod = run_product(rows, wave, mix, wave, 0, EARLY)
        row_even, row_odd = run_corner(flags, column_even, column_odd, own_even, own_odd, row_even, row_odd, prod[0])
        prod += run_product(rows, wave, mix, row_odd, EARLY, bands - EARLY)
        row_even = lax.ppermute(row_even, "gy", lat_even)
        row_odd = lax.ppermute(row_odd, ("gx", "gy"), lat_odd)
        out = run_block(
            last, index, rows, flags, state, *prod, row_even, row_odd, column_even, column_odd,
            own_even, own_odd, mix, side, gain, bias, forward, flipped, back, turn,
            expand, reduce,
        )
        if last:
            return out[0]
        state, *edges = out


def solution(mesh):
    return jax.shard_map(
        body,
        mesh=mesh,
        in_specs=(
            P(("gx", "gy"), None, None, None, None),
            P(None, ("gx", "gy")),
            P("gy", "gx"),
            P(),
            P(),
            P(),
            P(),
            P(),
            P(),
            P(),
        ),
        out_specs=P(None, "gy", "gx"),
        check_vma=False,
    )
```
